512 devices in a mesh: dp: 4 (over y), tm: 8 (over x, core), tile: 16 (over z).
Axes of the slice: x: 4, y: 4, z: 16, core: 2. Of those that a mesh axis runs over, the one named last changes fastest.
Arguments:
- frames_in: bfloat16 [4, 8, 48, 512, 128], P('dp', 'tm', None, 'tile'), may hold values from -6 to 6
- w_in: bfloat16 [96, 432], replicated, may hold values from -0.3125 to 0.3125
- gate_bias: float32 [48], replicated, may hold values from -1 to 3
- w_ent: bfloat16 [96, 864], replicated, may hold values from -0.21875 to 0.21875
- active_tiles: int32 [4, 8, 16, 12], P('dp', 'tm', 'tile'), may hold values from 0 to 15, as said below
- active_count: int32 [4, 8, 16], P('dp', 'tm', 'tile'), may hold values from 1 to 12, as said below
- cotangent: bfloat16 [4, 8, 16, 12, 48, 256], P('dp', 'tm', 'tile'), may hold values from -6 to 6
Outputs:
- latent: bfloat16 [4, 8, 16, 12, 48, 256], P('dp', 'tm', 'tile')
- weight_grad: float32 [96, 864], P('dp')
The draws below stay inside these ranges and needn't reach their ends.
Inputs may be any that keep to these rules, and one draw needn't show every extreme that they name: `active_tiles`: the entries of one band's list are different tile numbers; only the first active_count of them are used. `active_count`: in every clip and frame some band has 12 active tiles.
All inputs are finite; a program needn't handle non-finite values.
Results may differ from the reference program's by a relative error of at most 0.0038.
Values may be sent and summed in bfloat16 or wider, within the bound.
A program may use at most 64 MiB of HBM per device.

```python
import jax
import jax.numpy as jnp
from jax import lax

C = 48
ROWS = 32
COLS = 128
KMAX = 12
CLIPS = 4
FRAMES = 8
BANDS = 16
H = 512


def draw_active_tiles(key, part):
    key = jax.random.fold_in(key, 11)
    ntiles = ROWS // 16 * (COLS // 16)
    scores = jax.random.randint(key, (CLIPS, FRAMES, BANDS, ntiles), 0, 4096) * ntiles + jnp.arange(ntiles, dtype=jnp.int32)
    order = jnp.argsort(scores, axis=-1)
    return order[..., :KMAX].astype(jnp.int32)


def draw_active_count(key, part):
    key = jax.random.fold_in(key, 23)
    first, second = jax.random.split(key)
    base = jax.random.randint(first, (CLIPS, FRAMES, BANDS), 1, KMAX + 1)
    fullest = jax.random.randint(second, (CLIPS, FRAMES, 1), 0, BANDS)
    bands = jnp.arange(BANDS, dtype=jnp.int32)[None, None, :]
    return jnp.where(bands == fullest, KMAX, base).astype(jnp.int32)


def steps_of(own_key, dims, cuts, low, largest):
    def one(dim, parts):
        draws = jax.random.uniform(jax.random.fold_in(jax.random.fold_in(own_key, 6), dim), (parts,), jnp.float32, low / len(cuts), largest / len(cuts))
        return jnp.repeat(jnp.exp(draws), dims[dim] // parts).reshape((-1,) + (1,) * (len(dims) - dim - 1))

    loudness = one(*cuts[0])
    for cut in cuts[1:]:
        loudness = loudness * one(*cut)
    return loudness


def gaussian(stream_key, extent, deviation, bound, shards=(), kind=jnp.bfloat16):
    gain = steps_of(stream_key, extent, shards, -0.22, 0.18) if shards else 1.0
    drawn = jax.random.normal(stream_key, extent, jnp.float32) * deviation * gain
    return jnp.minimum(jnp.maximum(drawn, -bound), bound).astype(kind)


def setup_inputs(seed: int = 0) -> dict:
    seeds = jax.random.split(jax.random.key(seed), 8)
    frames_in = gaussian(seeds[0], (CLIPS, FRAMES, C, H, COLS), 1.0, 6.0, ((0, 4), (1, 8), (3, 16)))
    w_in = gaussian(seeds[1], (2 * C, 9 * C), (9 * C) ** -0.5, 0.3125)
    gate_bias = jnp.clip(jax.random.uniform(seeds[2], (C,), jnp.float32, -1.0, 3.0), -1.0, 3.0)
    w_ent = gaussian(seeds[3], (2 * C, 18 * C), (18 * C) ** -0.5, 0.21875)
    active_tiles = draw_active_tiles(jax.random.fold_in(seeds[7], 71), 0)
    active_count = draw_active_count(jax.random.fold_in(seeds[7], 71), 0)
    cotangent = gaussian(seeds[6], (CLIPS, FRAMES, BANDS, KMAX, C, 256), 1.0, 6.0, ((0, 4), (1, 8), (2, 16)))
    return dict(frames_in=frames_in, w_in=w_in, gate_bias=gate_bias, w_ent=w_ent, active_tiles=active_tiles, active_count=active_count, cotangent=cotangent)


def tile_patches(block):
    chans2 = block.shape[0]
    stacked = jnp.stack([block[:, dy:dy + 16, dx:dx + 16] for dy in range(3) for dx in range(3)])
    return stacked.reshape(9 * chans2, 256)


def entropy_terms(pre, target, cot, chans):
    mean = pre[:chans]
    spread = pre[chans:]
    sigma = 0.5 + jax.nn.softplus(spread)
    lat = (target - mean) / sigma
    push = jnp.concatenate([-cot / sigma, -cot * lat * jax.nn.sigmoid(spread) / sigma], axis=0)
    return lat, push


def reference(frames_in, w_in, gate_bias, w_ent, active_tiles, active_count, cotangent):
    nclip, nframe, chans, height, width = frames_in.shape
    flat = frames_in.reshape(nclip * nframe, chans, height, width)

    def input_conv(frame):
        padded = jnp.pad(frame, ((0, 0), (1, 1), (1, 1)))
        stacked = jnp.stack([padded[:, dy:dy + height, dx:dx + width] for dy in range(3) for dx in range(3)])
        mixed = jnp.dot(w_in, stacked.reshape(9 * chans, height * width), preferred_element_type=jnp.float32)
        gate = jax.nn.sigmoid(mixed[:chans] + gate_bias[:, None])
        drive = jnp.tanh(mixed[chans:])
        return gate, drive

    gates, drives = lax.map(input_conv, flat)
    gates = gates.reshape(nclip, nframe, chans, height * width)
    drives = drives.reshape(nclip, nframe, chans, height * width)
    state = jnp.zeros((nclip, chans, height * width), jnp.float32)
    contexts = []
    for frame_idx in range(nframe):
        contexts.append(state)
        state = gates[:, frame_idx] * state + drives[:, frame_idx]
    context = jnp.stack(contexts, axis=1).astype(jnp.bfloat16).reshape(nclip, nframe, chans, height, width)
    joined = jnp.concatenate([frames_in, context], axis=2)
    padded_all = jnp.pad(joined, ((0, 0), (0, 0), (0, 0), (1, 1), (1, 1)))
    nband = active_tiles.shape[2]
    kslots = active_tiles.shape[3]
    across = COLS // 16
    clip_ids = jnp.broadcast_to(jnp.arange(nclip, dtype=jnp.int32)[:, None, None, None], active_tiles.shape).reshape(-1)
    frame_ids = jnp.broadcast_to(jnp.arange(nframe, dtype=jnp.int32)[None, :, None, None], active_tiles.shape).reshape(-1)
    band_ids = jnp.broadcast_to(jnp.arange(nband, dtype=jnp.int32)[None, None, :, None], active_tiles.shape).reshape(-1)
    slot_ids = jnp.broadcast_to(jnp.arange(kslots, dtype=jnp.int32)[None, None, None, :], active_tiles.shape).reshape(-1)
    counts = jnp.broadcast_to(active_count[..., None], active_tiles.shape).reshape(-1)
    tiles = active_tiles.reshape(-1).astype(jnp.int32)
    cots = cotangent.reshape(-1, chans, 256)

    def step(grad, item):
        clip, frame, band, slot, ident, count, cot = item
        row0 = (band * ROWS + 16 * (ident // across)).astype(jnp.int32)
        col0 = (16 * (ident % across)).astype(jnp.int32)
        zero = jnp.int32(0)
        block = lax.dynamic_slice(padded_all, (clip, frame, zero, row0, col0), (1, 1, 2 * chans, 18, 18))[0, 0]
        patches = tile_patches(block)
        pre = jnp.dot(w_ent, patches, preferred_element_type=jnp.float32)
        target = lax.dynamic_slice(frames_in, (clip, frame, zero, row0, col0), (1, 1, chans, 16, 16))[0, 0]
        target = target.reshape(chans, 256).astype(jnp.float32)
        lat, push = entropy_terms(pre, target, cot.astype(jnp.float32), chans)
        live = (slot < count).astype(jnp.float32)
        push_bf = (push * live).astype(jnp.bfloat16)
        grad = grad + jnp.dot(push_bf, patches.T, preferred_element_type=jnp.float32)
        return grad, (lat * live).astype(jnp.bfloat16)

    init = jnp.zeros((2 * chans, 18 * chans), jnp.float32)
    grad, lats = lax.scan(step, init, (clip_ids, frame_ids, band_ids, slot_ids, tiles, counts, cots))
    latent = lats.reshape(nclip, nframe, nband, kslots, chans, 256)
    return latent, grad
```

```python
import functools

import jax
import jax.numpy as jnp
from jax import lax
from jax.experimental import pallas as pl
from jax.experimental.pallas import tpu as pltpu
from jax.sharding import PartitionSpec as P

BF = jnp.bfloat16
F32 = jnp.float32
MESH = pl.DeviceIdType.MESH


def z_groups(size):
    return [(1, 4), (4, 4)] if size == 16 else [(1, size)]


def swap_blocks(parts, lane):
    for m in (1, 2, 4):
        low = (lane & (16 * m)) == 0
        done = list(parts)
        for p in range(8):
            if p & m:
                continue
            q = p | m
            done[p] = jnp.where(low, parts[p], pltpu.roll(parts[q], 16 * m, 1))
            done[q] = jnp.where(low, pltpu.roll(parts[p], 128 - 16 * m, 1), parts[q])
        parts = done
    return parts


def store_shifts(out_ref, start, gap, value, lane):
    wide = value.astype(F32)
    before = jnp.where(lane == 0, 0.0, pltpu.roll(wide, 1, 1))
    after = jnp.where(lane == 127, 0.0, pltpu.roll(wide, 127, 1))
    out_ref[pl.ds(start, 48), :] = before.astype(BF)
    out_ref[pl.ds(start + gap, 48), :] = value
    out_ref[pl.ds(start + 2 * gap, 48), :] = after.astype(BF)


def kernel(
    sizes,
    x_hbm, w_in_ref, bias_ref, w_ent_ref, tiles_ref, count_ref, cot_hbm,
    lat_ref, grad_ref,
    xv, xf, xb, cotv, frame_rows, edge_rows, halo, conv_in, state, ctx_out, ctx, ctx_edge,
    joined, cot_dense, lat_dense, lat_tiles, grad_t, pieces, parts, z_out, z_in, final,
    load_sem, main_send, main_recv, edge_send, edge_recv, halo_send, halo_recv,
    ctx_send, ctx_recv, ctx_edge_send, ctx_edge_recv,
    piece_send, piece_recv, z_send, z_recv, final_send, final_recv,
):
    ydim, tdim, zdim = sizes
    y = lax.axis_index("dp")
    t = lax.axis_index("tm")
    b = lax.axis_index("tile")
    above = lax.rem(b + zdim - 1, zdim)
    below = lax.rem(b + 1, zdim)
    plane = ydim * tdim
    spot = y * tdim + t
    per = 32 // tdim
    groups = z_groups(zdim)
    out_rows = 96 // ydim
    pend = []

    def send(cond, make):
        @pl.when(cond)
        def _():
            make().start()

        pend.append((cond, make))

    def remote(src, dst, ssem, rsem, **where):
        return pltpu.make_async_remote_copy(
            src_ref=src, dst_ref=dst, send_sem=ssem, recv_sem=rsem, device_id=where, device_id_type=MESH
        )

    def arrived(ref, sem):
        pltpu.make_async_copy(ref, ref, sem).wait()

    def z_peer(stride, members, d):
        pos = lax.rem(b // stride, members)
        return b + (lax.rem(pos + d, members) - pos) * stride

    load_x = pltpu.make_async_copy(x_hbm, xv, load_sem.at[0])
    load_x.start()
    load_cot = pltpu.make_async_copy(cot_hbm, cotv, load_sem.at[1])
    load_cot.start()

    barrier = pltpu.get_barrier_semaphore()

    @pl.loop(1, plane)
    def _(d):
        peer = lax.rem(spot + d, plane)
        pl.semaphore_signal(
            barrier, inc=1, device_id={"dp": peer // tdim, "tm": lax.rem(peer, tdim)}, device_id_type=MESH
        )

    @pl.loop(0, tdim)
    def _(d):
        pl.semaphore_signal(barrier, inc=1, device_id={"tm": d, "tile": above}, device_id_type=MESH)
        pl.semaphore_signal(barrier, inc=1, device_id={"tm": d, "tile": below}, device_id_type=MESH)

    greeted = plane - 1 + 2 * tdim
    for stride, members in groups:
        for d in range(1, members):
            pl.semaphore_signal(
                barrier, inc=1, device_id={"tile": z_peer(stride, members, d)}, device_id_type=MESH
            )
            greeted += 1

    lane = lax.broadcasted_iota(jnp.int32, (48, 128), 1)
    blank = jnp.zeros((48, 128), BF)

    load_x.wait()
    xf[...] = xv[...].astype(F32).reshape(48 * 32, 128)
    xb[0] = blank
    xb[33] = blank
    for r in range(32):
        xb[1 + r] = xf[pl.ds(r, 48, stride=32), :].astype(BF)

    pl.semaphore_wait(barrier, greeted)

    sends = t < tdim - 1
    for j in range(tdim):
        send(
            sends & (t != j),
            lambda j=j: remote(
                xb.at[pl.ds(per * j, per + 2)], frame_rows.at[t], main_send.at[j], main_recv.at[t], tm=j
            ),
        )
    send(sends, lambda: remote(xb.at[32], edge_rows.at[t], edge_send.at[0], edge_recv.at[t], tm=0, tile=below))
    send(sends, lambda: remote(xb.at[1], edge_rows.at[t], edge_send.at[1], edge_recv.at[t], tm=tdim - 1, tile=above))
    always = t >= 0
    send(always, lambda: remote(xb.at[32], halo.at[0], halo_send.at[0], halo_recv.at[0], tile=below))
    send(always, lambda: remote(xb.at[1], halo.at[1], halo_send.at[1], halo_recv.at[1], tile=above))

    @pl.when(sends)
    def _():
        frame_rows[t] = xb[pl.ds(per * t, per + 2)]

    @pl.loop(1, 33)
    def _(r):
        store_shifts(joined, 288 * r, 96, xb[r], lane)

    load_cot.wait()
    count = count_ref[0]
    slots = []
    for n in range(16):
        found = jnp.int32(0)
        for k in range(12):
            found = jnp.where((tiles_ref[k] == n) & (k < count), k + 1, found)
        slots.append(found)
    for half in range(2):
        for h in range(2):
            columns = slice(128 * h, 128 * h + 128)
            rows = []
            for i in range(8):
                found = slots[8 * half + i]
                held = cotv[jnp.maximum(found - 1, 0), :, columns].astype(F32)
                rows.append(jnp.where(found > 0, held, 0.0))
            for i, row in enumerate(swap_blocks(rows, lane)):
                cot_dense[16 * half + 8 * h + i] = row

    for edge, row, there in ((0, 0, b > 0), (1, 33, b < zdim - 1)):
        arrived(halo.at[edge], halo_recv.at[edge])
        store_shifts(joined, 288 * row, 96, jnp.where(there, halo[edge], blank), lane)

    state[...] = jnp.zeros_like(state)

    @pl.loop(0, tdim - 1)
    def _(f):
        @pl.when(t != f)
        def _():
            arrived(frame_rows.at[f], main_recv.at[f])

        @pl.when(t == 0)
        def _():
            arrived(edge_rows.at[f], edge_recv.at[f])
            frame_rows[f, 0] = jnp.where(b > 0, edge_rows[f], blank)

        @pl.when(t == tdim - 1)
        def _():
            arrived(edge_rows.at[f], edge_recv.at[f])
            frame_rows[f, per + 1] = jnp.where(b < zdim - 1, edge_rows[f], blank)

        for r in range(per + 2):
            store_shifts(conv_in, 144 * r, 48, frame_rows[f, r], lane)
        taps = jnp.concatenate([conv_in[pl.ds(144 * r, 432), :] for r in range(per)], axis=1)
        mixed = jnp.dot(w_in_ref[...], taps, preferred_element_type=F32)
        gate = 0.5 * jnp.tanh(0.5 * (mixed[:48] + bias_ref[...])) + 0.5
        now = gate * state[...] + jnp.tanh(mixed[48:])
        state[...] = now
        for r in range(per):
            ctx_out[f, r] = now[:, 128 * r : 128 * r + 128].astype(BF)

        @pl.when(t != f + 1)
        def _():
            remote(
                ctx_out.at[f], ctx.at[pl.ds(1 + per * t, per)], ctx_send.at[f], ctx_recv.at[t], tm=f + 1
            ).start()

        @pl.when(t == f + 1)
        def _():
            ctx[pl.ds(1 + per * t, per)] = ctx_out[f]

        @pl.when(t == tdim - 1)
        def _():
            remote(
                ctx_out.at[f, per - 1], ctx_edge.at[0], ctx_edge_send.at[f], ctx_edge_recv.at[0],
                tm=f + 1, tile=below,
            ).start()

        @pl.when(t == 0)
        def _():
            remote(
                ctx_out.at[f, 0], ctx_edge.at[1], ctx_edge_send.at[f], ctx_edge_recv.at[1],
                tm=f + 1, tile=above,
            ).start()

    @pl.when(t == 0)
    def _():
        ctx[...] = jnp.zeros_like(ctx)
        ctx_edge[...] = jnp.zeros_like(ctx_edge)

    @pl.when(t > 0)
    def _():
        for j in range(tdim):
            @pl.when(t != j)
            def _():
                arrived(ctx.at[pl.ds(1 + per * j, per)], ctx_recv.at[j])
        for edge in range(2):
            arrived(ctx_edge.at[edge], ctx_edge_recv.at[edge])

    store_shifts(joined, 48, 96, jnp.where(b > 0, ctx_edge[0], blank), lane)
    store_shifts(joined, 288 * 33 + 48, 96, jnp.where(b < zdim - 1, ctx_edge[1], blank), lane)

    @pl.loop(1, 33)
    def _(r):
        store_shifts(joined, 288 * r + 48, 96, ctx[r], lane)

    grad_t[...] = jnp.zeros_like(grad_t)

    @pl.loop(0, 4)
    def _(part):
        base = 8 * part
        taps = jnp.concatenate([joined[pl.ds(288 * (base + r), 864), :] for r in range(8)], axis=1)
        pre = jnp.dot(w_ent_ref[...], taps, preferred_element_type=F32)
        pushes = []
        for r in range(8):
            mean = pre[:48, 128 * r : 128 * r + 128]
            spread = pre[48:, 128 * r : 128 * r + 128]
            small = jnp.exp(-jnp.abs(spread))
            sigma = 0.5 + jnp.maximum(spread, 0.0) + jnp.log(1.0 + small)
            slope = jnp.where(spread >= 0, 1.0, small) / (1.0 + small)
            scale = 1.0 / sigma
            lat = (xb[base + r + 1].astype(F32) - mean) * scale
            lat_dense[base + r] = lat
            near = -cot_dense[base + r] * scale
            pushes.append(jnp.concatenate([near, near * lat * slope], axis=0).astype(BF))
        push = jnp.concatenate(pushes, axis=1)
        grad_t[:864, :96] += lax.dot_general(taps, push, (((1,), (1,)), ((), ())), preferred_element_type=F32)

    for l in range(7):
        block = grad_t[128 * l : 128 * l + 128, :].T
        for other in range(ydim):
            pieces[7 * other + l, :out_rows] = block[out_rows * other : out_rows * (other + 1)].astype(BF)

    @pl.loop(1, plane)
    def _(d):
        peer = lax.rem(spot + d, plane)
        other, l = peer // tdim, lax.rem(peer, tdim)

        @pl.when(l < 7)
        def _():
            remote(pieces.at[7 * other + l], parts.at[spot], piece_send, piece_recv, dp=other, tm=l).start()

    for half in range(2):
        for h in range(2):
            rows = [lat_dense[16 * half + 8 * h + i] for i in range(8)]
            for i, row in enumerate(swap_blocks(rows, lane)):
                lat_tiles[8 * half + i, :, 128 * h : 128 * h + 128] = row.astype(BF)
    for k in range(12):
        held = lat_tiles[tiles_ref[k]]
        lat_ref[k] = jnp.where(k < count, held, jnp.zeros_like(held))

    owner = t < 7

    @pl.when(owner)
    def _():
        parts[spot] = pieces[7 * y + t]
        arrived(parts.at[pl.ds(0, plane - 1)], piece_recv)
        z_out[0] = jnp.zeros_like(z_out.at[0])

        @pl.loop(0, plane)
        def _(i):
            z_out[0] += parts[i].astype(F32)[:out_rows]

        for step, (stride, members) in enumerate(groups):
            for d in range(1, members):
                remote(
                    z_out.at[step], z_in.at[step, d - 1], z_send.at[step, d - 1], z_recv.at[step],
                    tile=z_peer(stride, members, d),
                ).start()
            arrived(z_in.at[step, pl.ds(0, members - 1)], z_recv.at[step])
            total = z_out[step]
            for d in range(1, members):
                total = total + z_in[step, d - 1]
            if step + 1 < len(groups):
                z_out[step + 1] = total
            else:
                final[t] = total
        for d in range(1, tdim):
            remote(
                final.at[t], final.at[t], final_send.at[d - 1], final_recv.at[t], tm=lax.rem(t + d, tdim)
            ).start()

    for l in range(7):
        @pl.when(t != l)
        def _():
            arrived(final.at[l], final_recv.at[l])

        width = min(128, 864 - 128 * l)
        grad_ref[:, 128 * l : 128 * l + width] = final[l][:, :width]

    for cond, make in pend:
        @pl.when(cond)
        def _(make=make):
            make().wait_send()

    @pl.loop(0, tdim - 1)
    def _(f):
        @pl.when(t != f + 1)
        def _():
            arrived(ctx_out.at[f], ctx_send.at[f])

        @pl.when((t == 0) | (t == tdim - 1))
        def _():
            arrived(ctx_out.at[f, 0], ctx_edge_send.at[f])

    @pl.when(owner)
    def _():
        arrived(pieces.at[pl.ds(0, 7 * ydim - 1)], piece_send)
        for step, (stride, members) in enumerate(groups):
            for d in range(1, members):
                arrived(z_out.at[step], z_send.at[step, d - 1])
        for d in range(1, tdim):
            arrived(final.at[t], final_send.at[d - 1])

    @pl.when(t == tdim - 1)
    def _():
        arrived(pieces, piece_send)


def body(sizes, frames_in, w_in, gate_bias, w_ent, active_tiles, active_count, cotangent):
    ydim, tdim, zdim = sizes
    plane = ydim * tdim
    per = 32 // tdim
    groups = z_groups(zdim)
    steps, most = len(groups), max(m for _, m in groups)
    out_rows = 96 // ydim
    held_rows = -(-out_rows // 16) * 16
    vmem = pl.BlockSpec(memory_space=pltpu.VMEM)
    smem = pl.BlockSpec(memory_space=pltpu.SMEM)
    hbm = pl.BlockSpec(memory_space=pl.ANY)
    dma = pltpu.SemaphoreType.DMA
    latent, grad = pl.pallas_call(
        functools.partial(kernel, sizes),
        out_shape=(
            jax.ShapeDtypeStruct((12, 48, 256), BF),
            jax.ShapeDtypeStruct((out_rows, 864), F32),
        ),
        in_specs=[hbm, vmem, vmem, vmem, smem, smem, hbm],
        out_specs=(vmem, vmem),
        scratch_shapes=[
            pltpu.VMEM((48, 32, 128), BF),
            pltpu.VMEM((48 * 32, 128), F32),
            pltpu.VMEM((34, 48, 128), BF),
            pltpu.VMEM((12, 48, 256), BF),
            pltpu.VMEM((tdim, per + 2, 48, 128), BF),
            pltpu.VMEM((tdim, 48, 128), BF),
            pltpu.VMEM((2, 48, 128), BF),
            pltpu.VMEM(((per + 2) * 144, 128), BF),
            pltpu.VMEM((48, per * 128), F32),
            pltpu.VMEM((tdim - 1, per, 48, 128), BF),
            pltpu.VMEM((34, 48, 128), BF),
            pltpu.VMEM((2, 48, 128), BF),
            pltpu.VMEM((34 * 288, 128), BF),
            pltpu.VMEM((32, 48, 128), F32),
            pltpu.VMEM((32, 48, 128), F32),
            pltpu.VMEM((16, 48, 256), BF),
            pltpu.VMEM((896, 128), F32),
            pltpu.VMEM((7 * ydim, held_rows, 128), BF),
            pltpu.VMEM((plane, held_rows, 128), BF),
            pltpu.VMEM((steps, out_rows, 128), F32),
            pltpu.VMEM((steps, most - 1, out_rows, 128), F32),
            pltpu.VMEM((7, out_rows, 128), F32),
            dma((2,)),
            dma((tdim,)), dma((tdim,)),
            dma((2,)), dma((tdim,)),
            dma((2,)), dma((2,)),
            dma((tdim - 1,)), dma((tdim,)),
            dma((tdim - 1,)), dma((2,)),
            dma, dma,
            dma((steps, most - 1)), dma((steps,)),
            dma((tdim - 1,)), dma((7,)),
        ],
        compiler_params=pltpu.CompilerParams(
            collective_id=0, has_side_effects=True, vmem_limit_bytes=32 * 1024 * 1024
        ),
        cost_estimate=pl.CostEstimate(flops=1_700_000_000, bytes_accessed=1_500_000, transcendentals=1_500_000),
        name="coding_window",
    )(
        frames_in[0, 0],
        w_in,
        gate_bias[:, None],
        w_ent,
        active_tiles[0, 0, 0],
        active_count[0, 0],
        cotangent[0, 0, 0],
    )
    return (latent[None, None, None], grad)


def solution(mesh):
    sizes = tuple(mesh.shape[axis] for axis in ("dp", "tm", "tile"))
    return jax.shard_map(
        functools.partial(body, sizes),
        mesh=mesh,
        in_specs=(
            P("dp", "tm", None, "tile", None),
            P(),
            P(),
            P(),
            P("dp", "tm", "tile", None),
            P("dp", "tm", "tile"),
            P("dp", "tm", "tile", None, None, None),
        ),
        out_specs=(P("dp", "tm", "tile", None, None, None), P("dp", None)),
        check_vma=False,
    )
```

```python
import functools

import jax
import jax.numpy as jnp
from jax import lax
from jax.experimental import pallas as pl
from jax.experimental.pallas import tpu as pltpu
from jax.sharding import PartitionSpec as P

BF = jnp.bfloat16
F32 = jnp.float32
MESH = pl.DeviceIdType.MESH


def z_steps(size):
    if size == 16:
        return [((1, 15, 14), True), ((2, 14, 6, 10), False)]
    return [(tuple(range(1, size)), True)]


def swap_blocks(parts, lane):
    for m in (1, 2, 4):
        low = (lane & (16 * m)) == 0
        done = list(parts)
        for p in range(8):
            if p & m:
                continue
            q = p | m
            done[p] = jnp.where(low, parts[p], pltpu.roll(parts[q], 16 * m, 1))
            done[q] = jnp.where(low, pltpu.roll(parts[p], 128 - 16 * m, 1), parts[q])
        parts = done
    return parts


def store_shifts(out_ref, start, gap, value, lane):
    wide = value.astype(F32)
    before = jnp.where(lane == 0, 0.0, pltpu.roll(wide, 1, 1))
    after = jnp.where(lane == 127, 0.0, pltpu.roll(wide, 127, 1))
    out_ref[pl.ds(start, 48), :] = before.astype(BF)
    out_ref[pl.ds(start + gap, 48), :] = value
    out_ref[pl.ds(start + 2 * gap, 48), :] = after.astype(BF)


def kernel(
    sizes,
    x_hbm, w_in_hbm, bias_hbm, w_ent_hbm, tiles_hbm, count_hbm, cot_hbm,
    lat_ref, grad_ref,
    w_in_ref, bias_ref, w_ent_ref, tiles_ref, count_ref,
    xv, xf, xb, cotv, frame_rows, edge_rows, halo, conv_in, state, ctx_out, ctx, ctx_edge,
    w_part, pre_x, joined, cot_dense, push, lat_dense, lat_tiles, grad_all, pieces, parts, z_out, z_in, final,
    load_sem, main_send, main_recv, edge_send, edge_recv, halo_send, halo_recv,
    ctx_send, ctx_recv, ctx_edge_send, ctx_edge_recv,
    piece_send, piece_recv, z_send, z_recv, final_send, final_recv,
):
    ydim, tdim, zdim = sizes
    y = lax.axis_index("dp")
    t = lax.axis_index("tm")
    b = lax.axis_index("tile")
    above = lax.rem(b + zdim - 1, zdim)
    below = lax.rem(b + 1, zdim)
    plane = ydim * tdim
    spot = y * tdim + t
    per = 32 // tdim
    steps = z_steps(zdim)
    out_rows = 96 // ydim
    pend = []

    def send(cond, make):
        @pl.when(cond)
        def _():
            make().start()

        pend.append((cond, make))

    def remote(src, dst, ssem, rsem, **where):
        return pltpu.make_async_remote_copy(
            src_ref=src, dst_ref=dst, send_sem=ssem, recv_sem=rsem, device_id=where, device_id_type=MESH
        )

    def arrived(ref, sem):
        pltpu.make_async_copy(ref, ref, sem).wait()

    loads = [
        pltpu.make_async_copy(src, dst, load_sem.at[i])
        for i, (src, dst) in enumerate(
            (
                (x_hbm, xv), (tiles_hbm, tiles_ref), (count_hbm, count_ref), (cot_hbm, cotv),
                (w_in_hbm, w_in_ref), (bias_hbm, bias_ref), (w_ent_hbm, w_ent_ref),
            )
        )
    ]
    for load in loads:
        load.start()

    barrier = pltpu.get_barrier_semaphore()

    @pl.loop(1, plane)
    def _(d):
        peer = lax.rem(spot + d, plane)
        pl.semaphore_signal(
            barrier, inc=1, device_id={"dp": peer // tdim, "tm": lax.rem(peer, tdim)}, device_id_type=MESH
        )

    @pl.loop(0, tdim)
    def _(d):
        pl.semaphore_signal(barrier, inc=1, device_id={"tm": d, "tile": above}, device_id_type=MESH)
        pl.semaphore_signal(barrier, inc=1, device_id={"tm": d, "tile": below}, device_id_type=MESH)

    greeted = plane - 1 + 2 * tdim
    for d in sorted({d for offsets, _ in steps for d in offsets} - {1, zdim - 1}):
        pl.semaphore_signal(barrier, inc=1, device_id={"tile": lax.rem(b + d, zdim)}, device_id_type=MESH)
        greeted += 1

    lane = lax.broadcasted_iota(jnp.int32, (48, 128), 1)
    blank = jnp.zeros((48, 128), BF)

    loads[0].wait()
    xf[...] = xv[...].astype(F32).reshape(48 * 32, 128)
    xb[0] = blank
    xb[33] = blank
    for r in range(32):
        xb[1 + r] = xf[pl.ds(r, 48, stride=32), :].astype(BF)

    pl.semaphore_wait(barrier, greeted)

    sends = t < tdim - 1
    send(sends, lambda: remote(xb.at[32], edge_rows.at[t], edge_send.at[0], edge_recv.at[t], tm=0, tile=below))
    send(sends, lambda: remote(xb.at[1], edge_rows.at[t], edge_send.at[1], edge_recv.at[t], tm=tdim - 1, tile=above))
    for d in range(1, tdim):
        j = lax.rem(t + d, tdim)
        send(
            sends,
            lambda d=d, j=j: remote(
                xb.at[pl.ds(per * j, per + 2)], frame_rows.at[t], main_send.at[d], main_recv.at[t], tm=j
            ),
        )
    always = t >= 0
    send(always, lambda: remote(xb.at[32], halo.at[0], halo_send.at[0], halo_recv.at[0], tile=below))
    send(always, lambda: remote(xb.at[1], halo.at[1], halo_send.at[1], halo_recv.at[1], tile=above))

    @pl.when(sends)
    def _():
        frame_rows[t] = xb[pl.ds(per * t, per + 2)]

    for r in range(1, 33):
        store_shifts(joined, 288 * r, 96, xb[r], lane)

    for load in loads[1:4]:
        load.wait()
    count = count_ref[0, 0, 0]
    slots = []
    for n in range(16):
        found = jnp.int32(0)
        for k in range(12):
            found = jnp.where((tiles_ref[0, k] == n) & (k < count), k + 1, found)
        slots.append(found)
    for half in range(2):
        for h in range(2):
            columns = slice(128 * h, 128 * h + 128)
            rows = []
            for i in range(8):
                found = slots[8 * half + i]
                held = cotv[jnp.maximum(found - 1, 0), :, columns].astype(F32)
                rows.append(jnp.where(found > 0, held, 0.0))
            for i, row in enumerate(swap_blocks(rows, lane)):
                cot_dense[16 * half + 8 * h + i] = row

    for edge, row, there in ((0, 0, b > 0), (1, 33, b < zdim - 1)):
        arrived(halo.at[edge], halo_recv.at[edge])
        store_shifts(joined, 288 * row, 96, jnp.where(there, halo[edge], blank), lane)

    loads[6].wait()
    w_all = w_ent_ref[...]
    for part in range(2):
        w_part[part] = jnp.concatenate([w_all[:, 96 * k + 48 * part : 96 * k + 48 * part + 48] for k in range(9)], axis=1)

    def taps(part, r):
        starts = [288 * (r + dy) + 96 * dx + 48 * part for dy in range(3) for dx in range(3)]
        return jnp.concatenate([joined[start : start + 48, :] for start in starts], axis=0)

    for block in range(2):
        cells = jnp.concatenate([taps(0, 16 * block + r) for r in range(16)], axis=1)
        pre_x[block] = jnp.dot(w_part[0], cells, preferred_element_type=F32)

    state[...] = jnp.zeros_like(state)
    for load in loads[4:6]:
        load.wait()
    bias = bias_ref[...].T[:48, :1]

    @pl.loop(0, tdim - 1)
    def _(f):
        @pl.when(t != f)
        def _():
            arrived(frame_rows.at[f], main_recv.at[f])

        @pl.when(t == 0)
        def _():
            arrived(edge_rows.at[f], edge_recv.at[f])
            frame_rows[f, 0] = jnp.where(b > 0, edge_rows[f], blank)

        @pl.when(t == tdim - 1)
        def _():
            arrived(edge_rows.at[f], edge_recv.at[f])
            frame_rows[f, per + 1] = jnp.where(b < zdim - 1, edge_rows[f], blank)

        for r in range(per + 2):
            store_shifts(conv_in, 144 * r, 48, frame_rows[f, r], lane)
        cells = jnp.concatenate([conv_in[pl.ds(144 * r, 432), :] for r in range(per)], axis=1)
        mixed = jnp.dot(w_in_ref[...], cells, preferred_element_type=F32)
        gate = 0.5 * jnp.tanh(0.5 * (mixed[:48] + bias)) + 0.5
        now = gate * state[...] + jnp.tanh(mixed[48:])
        state[...] = now
        for r in range(per):
            ctx_out[f, r] = now[:, 128 * r : 128 * r + 128].astype(BF)

        @pl.when(t != f + 1)
        def _():
            remote(
                ctx_out.at[f], ctx.at[pl.ds(1 + per * t, per)], ctx_send.at[f], ctx_recv.at[t], tm=f + 1
            ).start()

        @pl.when(t == f + 1)
        def _():
            ctx[pl.ds(1 + per * t, per)] = ctx_out[f]

        @pl.when(t == tdim - 1)
        def _():
            remote(
                ctx_out.at[f, per - 1], ctx_edge.at[0], ctx_edge_send.at[f], ctx_edge_recv.at[0],
                tm=f + 1, tile=below,
            ).start()

        @pl.when(t == 0)
        def _():
            remote(
                ctx_out.at[f, 0], ctx_edge.at[1], ctx_edge_send.at[f], ctx_edge_recv.at[1],
                tm=f + 1, tile=above,
            ).start()

    @pl.when(t == 0)
    def _():
        ctx[...] = jnp.zeros_like(ctx)
        ctx_edge[...] = jnp.zeros_like(ctx_edge)

    for j in range(tdim):
        @pl.when((t > 0) & (t != j))
        def _():
            arrived(ctx.at[pl.ds(1 + per * j, per)], ctx_recv.at[j])

        for r in range(1 + per * j, 1 + per * (j + 1)):
            store_shifts(joined, 288 * r + 48, 96, ctx[r], lane)

    for edge, row, there in ((0, 0, b > 0), (1, 33, b < zdim - 1)):
        @pl.when(t > 0)
        def _():
            arrived(ctx_edge.at[edge], ctx_edge_recv.at[edge])

        store_shifts(joined, 288 * row + 48, 96, jnp.where(there, ctx_edge[edge], blank), lane)

    for r in (-2, -1, 32, 33):
        push[96 * (33 - r) : 96 * (34 - r), :] = jnp.zeros((96, 128), BF)
    for block in range(2):
        cells = jnp.concatenate([taps(1, 16 * block + r) for r in range(16)], axis=1)
        pre = pre_x[block] + jnp.dot(w_part[1], cells, preferred_element_type=F32)
        for i in range(16):
            r = 16 * block + i
            mean = pre[:48, 128 * i : 128 * i + 128]
            spread = pre[48:, 128 * i : 128 * i + 128]
            small = jnp.exp(-jnp.abs(spread))
            sigma = 0.5 + jnp.maximum(spread, 0.0) + jnp.log(1.0 + small)
            slope = jnp.where(spread >= 0, 1.0, small) / (1.0 + small)
            scale = 1.0 / sigma
            lat = (xb[r + 1].astype(F32) - mean) * scale
            lat_dense[r] = lat
            near = -cot_dense[r] * scale
            push[96 * (33 - r) : 96 * (33 - r) + 48, :] = near.astype(BF)
            push[96 * (33 - r) + 48 : 96 * (34 - r), :] = (near * lat * slope).astype(BF)

    for first, last in ((0, 18), (18, 34)):
        near = jnp.concatenate([push[96 * (33 - r) : 96 * (36 - r), :] for r in range(first, last)], axis=1)
        rows = jnp.concatenate([joined[288 * r : 288 * r + 288, :] for r in range(first, last)], axis=1)
        term = lax.dot_general(near, rows, (((1,), (1,)), ((), ())), preferred_element_type=F32)
        if first == 0:
            grad_all[...] = term
        else:
            grad_all[...] += term

    for other in range(ydim):
        tails = []
        for dy in range(3):
            block = grad_all[96 * dy + out_rows * other : 96 * dy + out_rows * (other + 1), :]
            pieces[7 * other + 2 * dy, :out_rows] = block[:, :128].astype(BF)
            pieces[7 * other + 2 * dy + 1, :out_rows] = block[:, 128:256].astype(BF)
            tails.append(block[:, 256:])
        tails.append(jnp.zeros_like(tails[0]))
        pieces[7 * other + 6, :out_rows] = jnp.concatenate(tails, axis=1).astype(BF)

    @pl.loop(1, plane)
    def _(d):
        peer = lax.rem(spot + d, plane)
        other, l = peer // tdim, lax.rem(peer, tdim)

        @pl.when(l < 7)
        def _():
            remote(pieces.at[7 * other + l], parts.at[spot], piece_send, piece_recv, dp=other, tm=l).start()

    for half in range(2):
        for h in range(2):
            rows = [lat_dense[16 * half + 8 * h + i] for i in range(8)]
            for i, row in enumerate(swap_blocks(rows, lane)):
                lat_tiles[8 * half + i, :, 128 * h : 128 * h + 128] = row.astype(BF)
    for k in range(12):
        held = lat_tiles[tiles_ref[0, k]]
        lat_ref[k] = jnp.where(k < count, held, jnp.zeros_like(held))

    owner = t < 7

    @pl.when(owner)
    def _():
        parts[spot] = pieces[7 * y + t]
        arrived(parts.at[pl.ds(0, plane - 1)], piece_recv)
        total = jnp.zeros_like(z_out.at[0])
        for i in range(plane):
            total = total + parts[i].astype(F32)[:out_rows]
        z_out[0] = total

        for step, (offsets, own) in enumerate(steps):
            for i, d in enumerate(offsets):
                remote(
                    z_out.at[step], z_in.at[step, i], z_send.at[step, i], z_recv.at[step],
                    tile=lax.rem(b + d, zdim),
                ).start()
            arrived(z_in.at[step, pl.ds(0, len(offsets))], z_recv.at[step])
            total = z_out[step] if own else jnp.zeros_like(z_out.at[step])
            for i in range(len(offsets)):
                total = total + z_in[step, i]
            if step + 1 < len(steps):
                z_out[step + 1] = total
            else:
                final[t] = total
        for d in range(1, tdim):
            remote(
                final.at[t], final.at[t], final_send.at[d - 1], final_recv.at[t], tm=lax.rem(t + d, tdim)
            ).start()

    for l in range(7):
        @pl.when(t != l)
        def _():
            arrived(final.at[l], final_recv.at[l])

    for dy in range(3):
        grad_ref[:, 288 * dy : 288 * (dy + 1)] = jnp.concatenate(
            [final[2 * dy], final[2 * dy + 1], final[6][:, 32 * dy : 32 * (dy + 1)]], axis=1
        )

    for cond, make in pend:
        @pl.when(cond)
        def _(make=make):
            make().wait_send()

    @pl.loop(0, tdim - 1)
    def _(f):
        @pl.when(t != f + 1)
        def _():
            arrived(ctx_out.at[f], ctx_send.at[f])

        @pl.when((t == 0) | (t == tdim - 1))
        def _():
            arrived(ctx_out.at[f, 0], ctx_edge_send.at[f])

    @pl.when(owner)
    def _():
        arrived(pieces.at[pl.ds(0, 7 * ydim - 1)], piece_send)
        for step, (offsets, _) in enumerate(steps):
            for i in range(len(offsets)):
                arrived(z_out.at[step], z_send.at[step, i])
        for d in range(1, tdim):
            arrived(final.at[t], final_send.at[d - 1])

    @pl.when(t == tdim - 1)
    def _():
        arrived(pieces, piece_send)


def body(sizes, frames_in, w_in, gate_bias, w_ent, active_tiles, active_count, cotangent):
    ydim, tdim, zdim = sizes
    plane = ydim * tdim
    per = 32 // tdim
    steps = len(z_steps(zdim))
    most = max(len(offsets) for offsets, _ in z_steps(zdim))
    out_rows = 96 // ydim
    held_rows = -(-out_rows // 16) * 16
    vmem = pl.BlockSpec(memory_space=pltpu.VMEM)
    hbm = pl.BlockSpec(memory_space=pltpu.HBM)
    dma = pltpu.SemaphoreType.DMA
    latent, grad = pl.pallas_call(
        functools.partial(kernel, sizes),
        out_shape=(
            jax.ShapeDtypeStruct((12, 48, 256), BF),
            jax.ShapeDtypeStruct((out_rows, 864), F32),
        ),
        in_specs=[hbm] * 7,
        out_specs=(vmem, vmem),
        scratch_shapes=[
            pltpu.VMEM((96, 432), BF),
            pltpu.VMEM((1, 48), F32),
            pltpu.VMEM((96, 864), BF),
            pltpu.SMEM((1, 12), jnp.int32),
            pltpu.SMEM((1, 1, 1), jnp.int32),
            pltpu.VMEM((48, 32, 128), BF),
            pltpu.VMEM((48 * 32, 128), F32),
            pltpu.VMEM((34, 48, 128), BF),
            pltpu.VMEM((12, 48, 256), BF),
            pltpu.VMEM((tdim, per + 2, 48, 128), BF),
            pltpu.VMEM((tdim, 48, 128), BF),
            pltpu.VMEM((2, 48, 128), BF),
            pltpu.VMEM(((per + 2) * 144, 128), BF),
            pltpu.VMEM((48, per * 128), F32),
            pltpu.VMEM((tdim - 1, per, 48, 128), BF),
            pltpu.VMEM((34, 48, 128), BF),
            pltpu.VMEM((2, 48, 128), BF),
            pltpu.VMEM((2, 96, 432), BF),
            pltpu.VMEM((2, 96, 2048), F32),
            pltpu.VMEM((34 * 288, 128), BF),
            pltpu.VMEM((32, 48, 128), F32),
            pltpu.VMEM((36 * 96, 128), BF),
            pltpu.VMEM((32, 48, 128), F32),
            pltpu.VMEM((16, 48, 256), BF),
            pltpu.VMEM((288, 288), F32),
            pltpu.VMEM((7 * ydim, held_rows, 128), BF),
            pltpu.VMEM((plane, held_rows, 128), BF),
            pltpu.VMEM((steps, out_rows, 128), F32),
            pltpu.VMEM((steps, most, out_rows, 128), F32),
            pltpu.VMEM((7, out_rows, 128), F32),
            dma((7,)),
            dma((tdim,)), dma((tdim,)),
            dma((2,)), dma((tdim,)),
            dma((2,)), dma((2,)),
            dma((tdim - 1,)), dma((tdim,)),
            dma((tdim - 1,)), dma((2,)),
            dma, dma,
            dma((steps, most)), dma((steps,)),
            dma((tdim - 1,)), dma((7,)),
        ],
        compiler_params=pltpu.CompilerParams(
            collective_id=0, has_side_effects=True, vmem_limit_bytes=32 * 1024 * 1024
        ),
        cost_estimate=pl.CostEstimate(flops=1_700_000_000, bytes_accessed=1_500_000, transcendentals=1_500_000),
        name="coding_window",
    )(
        pltpu.with_memory_space_constraint(frames_in[0, 0], pltpu.HBM),
        pltpu.with_memory_space_constraint(w_in, pltpu.HBM),
        pltpu.with_memory_space_constraint(gate_bias[None], pltpu.HBM),
        pltpu.with_memory_space_constraint(w_ent, pltpu.HBM),
        pltpu.with_memory_space_constraint(active_tiles[0, 0], pltpu.HBM),
        active_count,
        pltpu.with_memory_space_constraint(cotangent[0, 0, 0], pltpu.HBM),
    )
    return (latent[None, None, None], grad)


def solution(mesh):
    sizes = tuple(mesh.shape[axis] for axis in ("dp", "tm", "tile"))
    return jax.shard_map(
        functools.partial(body, sizes),
        mesh=mesh,
        in_specs=(
            P("dp", "tm", None, "tile", None),
            P(),
            P(),
            P(),
            P("dp", "tm", "tile", None),
            P("dp", "tm", "tile"),
            P("dp", "tm", "tile", None, None, None),
        ),
        out_specs=(P("dp", "tm", "tile", None, None, None), P("dp", None)),
        check_vma=False,
    )
```

```python
import functools

import jax
import jax.numpy as jnp
from jax import lax
from jax.experimental import pallas as pl
from jax.experimental.pallas import tpu as pltpu
from jax.sharding import PartitionSpec as P

BF = jnp.bfloat16
F32 = jnp.float32
MESH = pl.DeviceIdType.MESH


REACH = 3


def relays(size):
    return max(0, -(-(size // 2) // REACH) - 1)


def swap_blocks(parts, lane):
    for m in (1, 2, 4):
        low = (lane & (16 * m)) == 0
        done = list(parts)
        for p in range(8):
            if p & m:
                continue
            q = p | m
            done[p] = jnp.where(low, parts[p], pltpu.roll(parts[q], 16 * m, 1))
            done[q] = jnp.where(low, pltpu.roll(parts[p], 128 - 16 * m, 1), parts[q])
        parts = done
    return parts


def store_shifts(out_ref, start, gap, value, lane):
    wide = value.astype(F32)
    before = jnp.where(lane == 0, 0.0, pltpu.roll(wide, 1, 1))
    after = jnp.where(lane == 127, 0.0, pltpu.roll(wide, 127, 1))
    out_ref[pl.ds(start, 48), :] = before.astype(BF)
    out_ref[pl.ds(start + gap, 48), :] = value
    out_ref[pl.ds(start + 2 * gap, 48), :] = after.astype(BF)


def kernel(
    sizes,
    x_hbm, w_in_hbm, bias_hbm, w_ent_hbm, tiles_hbm, count_hbm, cot_hbm,
    lat_ref, grad_ref,
    w_in_ref, bias_ref, w_ent_ref, tiles_ref, count_ref,
    xv, xf, xb, cotv, frame_rows, edge_rows, halo, conv_in, state, ctx_out, ctx, ctx_edge,
    w_part, pre_x, joined, cot_dense, push, lat_dense, lat_tiles, grad_all, pieces, parts, z_in, final,
    load_sem, main_send, main_recv, edge_send, edge_recv, halo_send, halo_recv,
    ctx_send, ctx_recv, ctx_edge_send, ctx_edge_recv,
    piece_send, piece_recv, z_send, z_recv, final_send, final_recv, relay_sem,
):
    ydim, tdim, zdim = sizes
    y = lax.axis_index("dp")
    t = lax.axis_index("tm")
    b = lax.axis_index("tile")
    above = lax.rem(b + zdim - 1, zdim)
    below = lax.rem(b + 1, zdim)
    plane = ydim * tdim
    spot = y * tdim + t
    per = 32 // tdim
    rounds = relays(zdim)
    out_rows = 96 // ydim
    pend = []

    def send(cond, make):
        @pl.when(cond)
        def _():
            make().start()

        pend.append((cond, make))

    def remote(src, dst, ssem, rsem, **where):
        return pltpu.make_async_remote_copy(
            src_ref=src, dst_ref=dst, send_sem=ssem, recv_sem=rsem, device_id=where, device_id_type=MESH
        )

    def arrived(ref, sem):
        pltpu.make_async_copy(ref, ref, sem).wait()

    loads = [
        pltpu.make_async_copy(src, dst, load_sem.at[i])
        for i, (src, dst) in enumerate(
            (
                (x_hbm, xv), (tiles_hbm, tiles_ref), (count_hbm, count_ref), (cot_hbm, cotv),
                (w_in_hbm, w_in_ref), (bias_hbm, bias_ref), (w_ent_hbm, w_ent_ref),
            )
        )
    ]
    for load in loads:
        load.start()

    barrier = pltpu.get_barrier_semaphore()

    @pl.loop(1, plane)
    def _(d):
        peer = lax.rem(spot + d, plane)
        pl.semaphore_signal(
            barrier, inc=1, device_id={"dp": peer // tdim, "tm": lax.rem(peer, tdim)}, device_id_type=MESH
        )

    @pl.loop(0, tdim)
    def _(d):
        pl.semaphore_signal(barrier, inc=1, device_id={"tm": d, "tile": above}, device_id_type=MESH)
        pl.semaphore_signal(barrier, inc=1, device_id={"tm": d, "tile": below}, device_id_type=MESH)

    greeted = plane - 1 + 2 * tdim
    for d in range(2, zdim - 1):
        if min(d, zdim - d) > REACH:
            continue
        pl.semaphore_signal(barrier, inc=1, device_id={"tile": lax.rem(b + d, zdim)}, device_id_type=MESH)
        greeted += 1

    lane = lax.broadcasted_iota(jnp.int32, (48, 128), 1)
    blank = jnp.zeros((48, 128), BF)

    loads[0].wait()
    xf[...] = xv[...].astype(F32).reshape(48 * 32, 128)
    xb[0] = blank
    xb[33] = blank
    for r in range(32):
        xb[1 + r] = xf[pl.ds(r, 48, stride=32), :].astype(BF)

    pl.semaphore_wait(barrier, greeted)

    def relay(step):
        for d in (REACH, zdim - REACH):
            pl.semaphore_signal(
                relay_sem.at[step], inc=1, device_id={"tile": lax.rem(b + d, zdim)}, device_id_type=MESH
            )

    if rounds > 0:
        relay(0)

    sends = t < tdim - 1
    send(sends, lambda: remote(xb.at[32], edge_rows.at[t], edge_send.at[0], edge_recv.at[t], tm=0, tile=below))
    send(sends, lambda: remote(xb.at[1], edge_rows.at[t], edge_send.at[1], edge_recv.at[t], tm=tdim - 1, tile=above))
    for d in range(1, tdim):
        j = lax.rem(t + d, tdim)
        send(
            sends,
            lambda d=d, j=j: remote(
                xb.at[pl.ds(per * j, per + 2)], frame_rows.at[t], main_send.at[d], main_recv.at[t], tm=j
            ),
        )
    always = t >= 0
    send(always, lambda: remote(xb.at[32], halo.at[0], halo_send.at[0], halo_recv.at[0], tile=below))
    send(always, lambda: remote(xb.at[1], halo.at[1], halo_send.at[1], halo_recv.at[1], tile=above))

    @pl.when(sends)
    def _():
        frame_rows[t] = xb[pl.ds(per * t, per + 2)]

    for r in range(1, 33):
        store_shifts(joined, 288 * r, 96, xb[r], lane)

    for load in loads[1:4]:
        load.wait()
    count = count_ref[0, 0, 0]
    slots = []
    for n in range(16):
        found = jnp.int32(0)
        for k in range(12):
            found = jnp.where((tiles_ref[0, k] == n) & (k < count), k + 1, found)
        slots.append(found)
    for half in range(2):
        for h in range(2):
            columns = slice(128 * h, 128 * h + 128)
            rows = []
            for i in range(8):
                found = slots[8 * half + i]
                held = cotv[jnp.maximum(found - 1, 0), :, columns].astype(F32)
                rows.append(jnp.where(found > 0, held, 0.0))
            for i, row in enumerate(swap_blocks(rows, lane)):
                cot_dense[16 * half + 8 * h + i] = row

    for edge, row, there in ((0, 0, b > 0), (1, 33, b < zdim - 1)):
        arrived(halo.at[edge], halo_recv.at[edge])
        store_shifts(joined, 288 * row, 96, jnp.where(there, halo[edge], blank), lane)

    loads[6].wait()
    w_all = w_ent_ref[...]
    for part in range(2):
        w_part[part] = jnp.concatenate([w_all[:, 96 * k + 48 * part : 96 * k + 48 * part + 48] for k in range(9)], axis=1)

    def taps(part, r):
        starts = [288 * (r + dy) + 96 * dx + 48 * part for dy in range(3) for dx in range(3)]
        return jnp.concatenate([joined[start : start + 48, :] for start in starts], axis=0)

    for block in range(2):
        cells = jnp.concatenate([taps(0, 16 * block + r) for r in range(16)], axis=1)
        pre_x[block] = jnp.dot(w_part[0], cells, preferred_element_type=F32)

    for step in range(1, rounds):
        pl.semaphore_wait(relay_sem.at[step - 1], 2)
        relay(step)

    state[...] = jnp.zeros_like(state)
    for load in loads[4:6]:
        load.wait()
    bias = bias_ref[...].T[:48, :1]

    @pl.loop(0, tdim - 1)
    def _(f):
        @pl.when(t != f)
        def _():
            arrived(frame_rows.at[f], main_recv.at[f])

        @pl.when(t == 0)
        def _():
            arrived(edge_rows.at[f], edge_recv.at[f])
            frame_rows[f, 0] = jnp.where(b > 0, edge_rows[f], blank)

        @pl.when(t == tdim - 1)
        def _():
            arrived(edge_rows.at[f], edge_recv.at[f])
            frame_rows[f, per + 1] = jnp.where(b < zdim - 1, edge_rows[f], blank)

        for r in range(per + 2):
            store_shifts(conv_in, 144 * r, 48, frame_rows[f, r], lane)
        cells = jnp.concatenate([conv_in[pl.ds(144 * r, 432), :] for r in range(per)], axis=1)
        mixed = jnp.dot(w_in_ref[...], cells, preferred_element_type=F32)
        gate = 0.5 * jnp.tanh(0.5 * (mixed[:48] + bias)) + 0.5
        now = gate * state[...] + jnp.tanh(mixed[48:])
        state[...] = now
        for r in range(per):
            ctx_out[f, r] = now[:, 128 * r : 128 * r + 128].astype(BF)

        @pl.when(t != f + 1)
        def _():
            remote(
                ctx_out.at[f], ctx.at[pl.ds(1 + per * t, per)], ctx_send.at[f], ctx_recv.at[t], tm=f + 1
            ).start()

        @pl.when(t == f + 1)
        def _():
            ctx[pl.ds(1 + per * t, per)] = ctx_out[f]

        @pl.when(t == tdim - 1)
        def _():
            remote(
                ctx_out.at[f, per - 1], ctx_edge.at[0], ctx_edge_send.at[f], ctx_edge_recv.at[0],
                tm=f + 1, tile=below,
            ).start()

        @pl.when(t == 0)
        def _():
            remote(
                ctx_out.at[f, 0], ctx_edge.at[1], ctx_edge_send.at[f], ctx_edge_recv.at[1],
                tm=f + 1, tile=above,
            ).start()

    if rounds > 0:
        pl.semaphore_wait(relay_sem.at[rounds - 1], 2)

    @pl.when(t == 0)
    def _():
        ctx[...] = jnp.zeros_like(ctx)
        ctx_edge[...] = jnp.zeros_like(ctx_edge)

    for j in range(tdim):
        @pl.when((t > 0) & (t != j))
        def _():
            arrived(ctx.at[pl.ds(1 + per * j, per)], ctx_recv.at[j])

        for r in range(1 + per * j, 1 + per * (j + 1)):
            store_shifts(joined, 288 * r + 48, 96, ctx[r], lane)

    for edge, row, there in ((0, 0, b > 0), (1, 33, b < zdim - 1)):
        @pl.when(t > 0)
        def _():
            arrived(ctx_edge.at[edge], ctx_edge_recv.at[edge])

        store_shifts(joined, 288 * row + 48, 96, jnp.where(there, ctx_edge[edge], blank), lane)

    for r in (-2, -1, 32, 33):
        push[96 * (33 - r) : 96 * (34 - r), :] = jnp.zeros((96, 128), BF)
    for block in range(2):
        cells = jnp.concatenate([taps(1, 16 * block + r) for r in range(16)], axis=1)
        pre = pre_x[block] + jnp.dot(w_part[1], cells, preferred_element_type=F32)
        for i in range(16):
            r = 16 * block + i
            mean = pre[:48, 128 * i : 128 * i + 128]
            spread = pre[48:, 128 * i : 128 * i + 128]
            small = jnp.exp(-jnp.abs(spread))
            sigma = 0.5 + jnp.maximum(spread, 0.0) + jnp.log(1.0 + small)
            slope = jnp.where(spread >= 0, 1.0, small) / (1.0 + small)
            scale = 1.0 / sigma
            lat = (xb[r + 1].astype(F32) - mean) * scale
            lat_dense[r] = lat
            near = -cot_dense[r] * scale
            push[96 * (33 - r) : 96 * (33 - r) + 48, :] = near.astype(BF)
            push[96 * (33 - r) + 48 : 96 * (34 - r), :] = (near * lat * slope).astype(BF)

    for first, last in ((0, 18), (18, 34)):
        near = jnp.concatenate([push[96 * (33 - r) : 96 * (36 - r), :] for r in range(first, last)], axis=1)
        rows = jnp.concatenate([joined[288 * r : 288 * r + 288, :] for r in range(first, last)], axis=1)
        term = lax.dot_general(near, rows, (((1,), (1,)), ((), ())), preferred_element_type=F32)
        if first == 0:
            grad_all[...] = term
        else:
            grad_all[...] += term

    for other in range(ydim):
        tails = []
        for dy in range(3):
            block = grad_all[96 * dy + out_rows * other : 96 * dy + out_rows * (other + 1), :]
            pieces[7 * other + 2 * dy, :out_rows] = block[:, :128].astype(BF)
            pieces[7 * other + 2 * dy + 1, :out_rows] = block[:, 128:256].astype(BF)
            tails.append(block[:, 256:])
        tails.append(jnp.zeros_like(tails[0]))
        pieces[7 * other + 6, :out_rows] = jnp.concatenate(tails, axis=1).astype(BF)

    @pl.loop(1, plane)
    def _(d):
        peer = lax.rem(spot + d, plane)
        other, l = peer // tdim, lax.rem(peer, tdim)

        @pl.when(l < 7)
        def _():
            remote(pieces.at[7 * other + l], parts.at[spot], piece_send, piece_recv, dp=other, tm=l).start()

    for half in range(2):
        for h in range(2):
            rows = [lat_dense[16 * half + 8 * h + i] for i in range(8)]
            for i, row in enumerate(swap_blocks(rows, lane)):
                lat_tiles[8 * half + i, :, 128 * h : 128 * h + 128] = row.astype(BF)
    for k in range(12):
        held = lat_tiles[tiles_ref[0, k]]
        lat_ref[k] = jnp.where(k < count, held, jnp.zeros_like(held))

    owner = t < 7

    @pl.when(owner)
    def _():
        parts[spot] = pieces[7 * y + t]
        arrived(parts.at[pl.ds(0, plane - 1)], piece_recv)
        total = parts[0].astype(F32)
        for i in range(1, plane):
            total = total + parts[i].astype(F32)
        z_in[b] = total.astype(BF)
        for d in sorted(range(1, zdim), key=lambda d: -min(d, zdim - d)):
            remote(z_in.at[b], z_in.at[b], z_send.at[d], z_recv, tile=lax.rem(b + d, zdim)).start()
        arrived(z_in.at[pl.ds(0, zdim - 1)], z_recv)
        total = z_in[0].astype(F32)
        for i in range(1, zdim):
            total = total + z_in[i].astype(F32)
        final[t] = total[:out_rows]
        for d in range(1, tdim):
            remote(
                final.at[t], final.at[t], final_send.at[d - 1], final_recv.at[t], tm=lax.rem(t + d, tdim)
            ).start()

    for l in range(7):
        @pl.when(t != l)
        def _():
            arrived(final.at[l], final_recv.at[l])

    for dy in range(3):
        grad_ref[:, 288 * dy : 288 * (dy + 1)] = jnp.concatenate(
            [final[2 * dy], final[2 * dy + 1], final[6][:, 32 * dy : 32 * (dy + 1)]], axis=1
        )

    for cond, make in pend:
        @pl.when(cond)
        def _(make=make):
            make().wait_send()

    @pl.loop(0, tdim - 1)
    def _(f):
        @pl.when(t != f + 1)
        def _():
            arrived(ctx_out.at[f], ctx_send.at[f])

        @pl.when((t == 0) | (t == tdim - 1))
        def _():
            arrived(ctx_out.at[f, 0], ctx_edge_send.at[f])

    @pl.when(owner)
    def _():
        arrived(pieces.at[pl.ds(0, 7 * ydim - 1)], piece_send)
        for d in range(1, zdim):
            arrived(z_in.at[b], z_send.at[d])
        for d in range(1, tdim):
            arrived(final.at[t], final_send.at[d - 1])

    @pl.when(t == tdim - 1)
    def _():
        arrived(pieces, piece_send)


def body(sizes, frames_in, w_in, gate_bias, w_ent, active_tiles, active_count, cotangent):
    ydim, tdim, zdim = sizes
    plane = ydim * tdim
    per = 32 // tdim
    out_rows = 96 // ydim
    held_rows = -(-out_rows // 16) * 16
    vmem = pl.BlockSpec(memory_space=pltpu.VMEM)
    hbm = pl.BlockSpec(memory_space=pltpu.HBM)
    dma = pltpu.SemaphoreType.DMA
    latent, grad = pl.pallas_call(
        functools.partial(kernel, sizes),
        out_shape=(
            jax.ShapeDtypeStruct((12, 48, 256), BF),
            jax.ShapeDtypeStruct((out_rows, 864), F32),
        ),
        in_specs=[hbm] * 7,
        out_specs=(vmem, vmem),
        scratch_shapes=[
            pltpu.VMEM((96, 432), BF),
            pltpu.VMEM((1, 48), F32),
            pltpu.VMEM((96, 864), BF),
            pltpu.SMEM((1, 12), jnp.int32),
            pltpu.SMEM((1, 1, 1), jnp.int32),
            pltpu.VMEM((48, 32, 128), BF),
            pltpu.VMEM((48 * 32, 128), F32),
            pltpu.VMEM((34, 48, 128), BF),
            pltpu.VMEM((12, 48, 256), BF),
            pltpu.VMEM((tdim, per + 2, 48, 128), BF),
            pltpu.VMEM((tdim, 48, 128), BF),
            pltpu.VMEM((2, 48, 128), BF),
            pltpu.VMEM(((per + 2) * 144, 128), BF),
            pltpu.VMEM((48, per * 128), F32),
            pltpu.VMEM((tdim - 1, per, 48, 128), BF),
            pltpu.VMEM((34, 48, 128), BF),
            pltpu.VMEM((2, 48, 128), BF),
            pltpu.VMEM((2, 96, 432), BF),
            pltpu.VMEM((2, 96, 2048), F32),
            pltpu.VMEM((34 * 288, 128), BF),
            pltpu.VMEM((32, 48, 128), F32),
            pltpu.VMEM((36 * 96, 128), BF),
            pltpu.VMEM((32, 48, 128), F32),
            pltpu.VMEM((16, 48, 256), BF),
            pltpu.VMEM((288, 288), F32),
            pltpu.VMEM((7 * ydim, held_rows, 128), BF),
            pltpu.VMEM((plane, held_rows, 128), BF),
            pltpu.VMEM((zdim, held_rows, 128), BF),
            pltpu.VMEM((7, out_rows, 128), F32),
            dma((7,)),
            dma((tdim,)), dma((tdim,)),
            dma((2,)), dma((tdim,)),
            dma((2,)), dma((2,)),
            dma((tdim - 1,)), dma((tdim,)),
            dma((tdim - 1,)), dma((2,)),
            dma, dma,
            dma((zdim,)), dma,
            dma((tdim - 1,)), dma((7,)),
            pltpu.SemaphoreType.REGULAR((max(1, relays(zdim)),)),
        ],
        compiler_params=pltpu.CompilerParams(
            collective_id=0, has_side_effects=True, vmem_limit_bytes=32 * 1024 * 1024
        ),
        cost_estimate=pl.CostEstimate(flops=1_700_000_000, bytes_accessed=1_500_000, transcendentals=1_500_000),
        name="coding_window",
    )(
        pltpu.with_memory_space_constraint(frames_in[0, 0], pltpu.HBM),
        pltpu.with_memory_space_constraint(w_in, pltpu.HBM),
        pltpu.with_memory_space_constraint(gate_bias[None], pltpu.HBM),
        pltpu.with_memory_space_constraint(w_ent, pltpu.HBM),
        pltpu.with_memory_space_constraint(active_tiles[0, 0], pltpu.HBM),
        active_count,
        pltpu.with_memory_space_constraint(cotangent[0, 0, 0], pltpu.HBM),
    )
    return (latent[None, None, None], grad)


def solution(mesh):
    sizes = tuple(mesh.shape[axis] for axis in ("dp", "tm", "tile"))
    return jax.shard_map(
        functools.partial(body, sizes),
        mesh=mesh,
        in_specs=(
            P("dp", "tm", None, "tile", None),
            P(),
            P(),
            P(),
            P("dp", "tm", "tile", None),
            P("dp", "tm", "tile"),
            P("dp", "tm", "tile", None, None, None),
        ),
        out_specs=(P("dp", "tm", "tile", None, None, None), P("dp", None)),
        check_vma=False,
    )
```

```python
import functools

import jax
import jax.numpy as jnp
from jax import lax
from jax.experimental import pallas as pl
from jax.experimental.pallas import tpu as pltpu
from jax.sharding import PartitionSpec as P

BF = jnp.bfloat16
F32 = jnp.float32
MESH = pl.DeviceIdType.MESH


NEAR = 2


def relay_strides(size):
    strides, known = [], NEAR
    while known < size // 2:
        strides.append(known)
        known *= 2
    return strides


def swap_blocks(parts, lane):
    for m in (1, 2, 4):
        low = (lane & (16 * m)) == 0
        done = list(parts)
        for p in range(8):
            if p & m:
                continue
            q = p | m
            done[p] = jnp.where(low, parts[p], pltpu.roll(parts[q], 16 * m, 1))
            done[q] = jnp.where(low, pltpu.roll(parts[p], 128 - 16 * m, 1), parts[q])
        parts = done
    return parts


def store_shifts(out_ref, start, gap, value, lane):
    wide = value.astype(F32)
    before = jnp.where(lane == 0, 0.0, pltpu.roll(wide, 1, 1))
    after = jnp.where(lane == 127, 0.0, pltpu.roll(wide, 127, 1))
    out_ref[pl.ds(start, 48), :] = before.astype(BF)
    out_ref[pl.ds(start + gap, 48), :] = value
    out_ref[pl.ds(start + 2 * gap, 48), :] = after.astype(BF)


def kernel(
    sizes,
    x_hbm, w_in_hbm, bias_hbm, w_ent_hbm, tiles_hbm, count_hbm, cot_hbm,
    lat_ref, grad_ref,
    w_in_ref, bias_ref, w_ent_ref, tiles_ref, count_ref,
    xv, xf, xb, cotv, frame_rows, edge_rows, halo, conv_in, gates, drives, state, ctx_out, ctx, ctx_edge,
    w_part, pre_x, joined, cot_dense, push, lat_dense, lat_tiles, grad_all, pieces, parts, z_in, final,
    load_sem, main_send, main_recv, edge_send, edge_recv, halo_send, halo_recv,
    ctx_send, ctx_recv, ctx_edge_send, ctx_edge_recv,
    piece_send, piece_recv, z_send, z_recv, final_send, final_recv, relay_sem,
):
    ydim, tdim, zdim = sizes
    y = lax.axis_index("dp")
    t = lax.axis_index("tm")
    b = lax.axis_index("tile")
    above = lax.rem(b + zdim - 1, zdim)
    below = lax.rem(b + 1, zdim)
    plane = ydim * tdim
    spot = y * tdim + t
    per = 32 // tdim
    strides = relay_strides(zdim)
    out_rows = 96 // ydim
    pend = []

    def send(cond, make):
        @pl.when(cond)
        def _():
            make().start()

        pend.append((cond, make))

    def remote(src, dst, ssem, rsem, **where):
        return pltpu.make_async_remote_copy(
            src_ref=src, dst_ref=dst, send_sem=ssem, recv_sem=rsem, device_id=where, device_id_type=MESH
        )

    def arrived(ref, sem):
        pltpu.make_async_copy(ref, ref, sem).wait()

    loads = [
        pltpu.make_async_copy(src, dst, load_sem.at[i])
        for i, (src, dst) in enumerate(
            (
                (x_hbm, xv), (tiles_hbm, tiles_ref), (count_hbm, count_ref), (cot_hbm, cotv),
                (w_in_hbm, w_in_ref), (bias_hbm, bias_ref), (w_ent_hbm, w_ent_ref),
            )
        )
    ]
    for load in loads:
        load.start()

    barrier = pltpu.get_barrier_semaphore()

    greeted = 0
    for axis, size, offsets in (
        ("tm", tdim, range(1, tdim)),
        ("tile", zdim, [d for d in range(1, zdim) if min(d, zdim - d) <= NEAR]),
        ("dp", ydim, range(1, ydim)),
    ):
        for d in offsets:
            peer = lax.rem(lax.axis_index(axis) + d, size)
            pl.semaphore_signal(barrier, inc=1, device_id={axis: peer}, device_id_type=MESH)
            greeted += 1

    lane = lax.broadcasted_iota(jnp.int32, (48, 128), 1)
    blank = jnp.zeros((48, 128), BF)

    loads[0].wait()
    xf[...] = xv[...].astype(F32).reshape(48 * 32, 128)
    xb[0] = blank
    xb[33] = blank
    for r in range(32):
        xb[1 + r] = xf[pl.ds(r, 48, stride=32), :].astype(BF)

    pl.semaphore_wait(barrier, greeted)

    def relay(step, axis, size, offsets):
        for d in offsets:
            peer = lax.rem(lax.axis_index(axis) + d, size)
            pl.semaphore_signal(relay_sem.at[step], inc=1, device_id={axis: peer}, device_id_type=MESH)

    sends = t < tdim - 1
    always = t >= 0
    send(always, lambda: remote(xb.at[32], halo.at[0], halo_send.at[0], halo_recv.at[0], tile=below))
    send(always, lambda: remote(xb.at[1], halo.at[1], halo_send.at[1], halo_recv.at[1], tile=above))
    for d in range(1, tdim):
        j = lax.rem(t + tdim - d, tdim)
        send(
            sends,
            lambda d=d, j=j: remote(
                xb.at[pl.ds(per * j, per + 2)], frame_rows.at[t], main_send.at[d], main_recv.at[t], tm=j
            ),
        )
    relay(len(strides), "dp", ydim, range(1, ydim))
    if strides:
        relay(0, "tile", zdim, (strides[0], zdim - strides[0]))

    @pl.when(sends)
    def _():
        frame_rows[t] = xb[pl.ds(per * t, per + 2)]

    for r in range(1, 33):
        store_shifts(joined, 288 * r, 96, xb[r], lane)

    for load in loads[1:4]:
        load.wait()
    count = count_ref[0, 0, 0]
    slots = []
    for n in range(16):
        found = jnp.int32(0)
        for k in range(12):
            found = jnp.where((tiles_ref[0, k] == n) & (k < count), k + 1, found)
        slots.append(found)
    for half in range(2):
        for h in range(2):
            columns = slice(128 * h, 128 * h + 128)
            rows = []
            for i in range(8):
                found = slots[8 * half + i]
                held = cotv[jnp.maximum(found - 1, 0), :, columns].astype(F32)
                rows.append(jnp.where(found > 0, held, 0.0))
            for i, row in enumerate(swap_blocks(rows, lane)):
                cot_dense[16 * half + 8 * h + i] = row

    for edge, row, there in ((0, 0, b > 0), (1, 33, b < zdim - 1)):
        arrived(halo.at[edge], halo_recv.at[edge])
        end = edge * (tdim - 1)
        send(
            sends & (t != end),
            lambda edge=edge, end=end: remote(
                halo.at[edge], edge_rows.at[t], edge_send.at[edge], edge_recv.at[t], tm=end
            ),
        )
        store_shifts(joined, 288 * row, 96, jnp.where(there, halo[edge], blank), lane)

    @pl.when(t == 0)
    def _():
        edge_rows[0] = halo[0]

    loads[6].wait()
    w_all = w_ent_ref[...]
    for part in range(2):
        w_part[part] = jnp.concatenate([w_all[:, 96 * k + 48 * part : 96 * k + 48 * part + 48] for k in range(9)], axis=1)

    def taps(part, r):
        starts = [288 * (r + dy) + 96 * dx + 48 * part for dy in range(3) for dx in range(3)]
        return jnp.concatenate([joined[start : start + 48, :] for start in starts], axis=0)

    for block in range(2):
        cells = jnp.concatenate([taps(0, 16 * block + r) for r in range(16)], axis=1)
        pre_x[block] = jnp.dot(w_part[0], cells, preferred_element_type=F32)

    for step in range(1, len(strides)):
        pl.semaphore_wait(relay_sem.at[step - 1], 2)
        relay(step, "tile", zdim, (strides[step], zdim - strides[step]))

    state[...] = jnp.zeros_like(state)
    for load in loads[4:6]:
        load.wait()
    bias = bias_ref[...].T[:48, :1]

    def convolve(f):
        @pl.when(t != f)
        def _():
            arrived(frame_rows.at[f], main_recv.at[f])

        for end, row, there in ((0, 0, b > 0), (tdim - 1, per + 1, b < zdim - 1)):
            @pl.when(t == end)
            def _():
                @pl.when(f != end)
                def _():
                    arrived(edge_rows.at[f], edge_recv.at[f])

                frame_rows[f, row] = jnp.where(there, edge_rows[f], blank)

        for r in range(per + 2):
            store_shifts(conv_in, 144 * r, 48, frame_rows[f, r], lane)
        cells = jnp.concatenate([conv_in[pl.ds(144 * r, 432), :] for r in range(per)], axis=1)
        mixed = jnp.dot(w_in_ref[...], cells, preferred_element_type=F32)
        gates[f] = 0.5 * jnp.tanh(0.5 * (mixed[:48] + bias)) + 0.5
        drives[f] = jnp.tanh(mixed[48:])

    def advance(f):
        now = gates[f] * state[...] + drives[f]
        state[...] = now
        for r in range(per):
            ctx_out[f, r] = now[:, 128 * r : 128 * r + 128].astype(BF)

        @pl.when(t != f + 1)
        def _():
            remote(
                ctx_out.at[f], ctx.at[pl.ds(1 + per * t, per)], ctx_send.at[f], ctx_recv.at[t], tm=f + 1
            ).start()

        @pl.when(t == f + 1)
        def _():
            ctx[pl.ds(1 + per * t, per)] = ctx_out[f]

        @pl.when(t == tdim - 1)
        def _():
            remote(
                ctx_out.at[f, per - 1], ctx_edge.at[0], ctx_edge_send.at[f], ctx_edge_recv.at[0],
                tm=f + 1, tile=below,
            ).start()

        @pl.when(t == 0)
        def _():
            remote(
                ctx_out.at[f, 0], ctx_edge.at[1], ctx_edge_send.at[f], ctx_edge_recv.at[1],
                tm=f + 1, tile=above,
            ).start()

    @pl.loop(0, tdim)
    def _(i):
        f = lax.rem(t + i, tdim)

        @pl.when(f < tdim - 1)
        def _():
            convolve(f)

            @pl.when((f < t) | (t == 0))
            def _():
                advance(f)

    @pl.loop(0, tdim - 1)
    def _(f):
        @pl.when((f >= t) & (t > 0))
        def _():
            advance(f)

    if strides:
        pl.semaphore_wait(relay_sem.at[len(strides) - 1], 2)
    if ydim > 1:
        pl.semaphore_wait(relay_sem.at[len(strides)], ydim - 1)

    @pl.when(t == 0)
    def _():
        ctx[...] = jnp.zeros_like(ctx)
        ctx_edge[...] = jnp.zeros_like(ctx_edge)

    for j in range(tdim):
        @pl.when((t > 0) & (t != j))
        def _():
            arrived(ctx.at[pl.ds(1 + per * j, per)], ctx_recv.at[j])

        for r in range(1 + per * j, 1 + per * (j + 1)):
            store_shifts(joined, 288 * r + 48, 96, ctx[r], lane)

    for edge, row, there in ((0, 0, b > 0), (1, 33, b < zdim - 1)):
        @pl.when(t > 0)
        def _():
            arrived(ctx_edge.at[edge], ctx_edge_recv.at[edge])

        store_shifts(joined, 288 * row + 48, 96, jnp.where(there, ctx_edge[edge], blank), lane)

    for r in (-2, -1, 32, 33):
        push[96 * (33 - r) : 96 * (34 - r), :] = jnp.zeros((96, 128), BF)
    for block in range(2):
        cells = jnp.concatenate([taps(1, 16 * block + r) for r in range(16)], axis=1)
        pre = pre_x[block] + jnp.dot(w_part[1], cells, preferred_element_type=F32)
        for i in range(16):
            r = 16 * block + i
            mean = pre[:48, 128 * i : 128 * i + 128]
            spread = pre[48:, 128 * i : 128 * i + 128]
            small = jnp.exp(-jnp.abs(spread))
            sigma = 0.5 + jnp.maximum(spread, 0.0) + jnp.log(1.0 + small)
            slope = jnp.where(spread >= 0, 1.0, small) / (1.0 + small)
            scale = 1.0 / sigma
            lat = (xb[r + 1].astype(F32) - mean) * scale
            lat_dense[r] = lat
            near = -cot_dense[r] * scale
            push[96 * (33 - r) : 96 * (33 - r) + 48, :] = near.astype(BF)
            push[96 * (33 - r) + 48 : 96 * (34 - r), :] = (near * lat * slope).astype(BF)

    near = jnp.concatenate([push[96 * (33 - r) : 96 * (36 - r), :] for r in range(34)], axis=1)

    def gradient(first, last):
        rows = jnp.concatenate([joined[288 * r + first : 288 * r + last, :] for r in range(34)], axis=1)
        return lax.dot_general(near, rows, (((1,), (1,)), ((), ())), preferred_element_type=F32)

    def send_piece(other, l):
        remote(pieces.at[7 * other + l], parts.at[spot], piece_send, piece_recv, dp=other, tm=l).start()

    grad_all[...] = gradient(0, 256)
    for other in range(ydim):
        for dy in range(3):
            block = grad_all[96 * dy + out_rows * other : 96 * dy + out_rows * (other + 1), :]
            pieces[7 * other + 2 * dy, :out_rows] = block[:, :128].astype(BF)
            pieces[7 * other + 2 * dy + 1, :out_rows] = block[:, 128:].astype(BF)

    @pl.loop(1, plane)
    def _(d):
        peer = lax.rem(spot + d, plane)
        other, l = peer // tdim, lax.rem(peer, tdim)

        @pl.when(l < 6)
        def _():
            send_piece(other, l)

    grad_all[:, :32] = gradient(256, 288)
    for other in range(ydim):
        tails = [grad_all[96 * dy + out_rows * other : 96 * dy + out_rows * (other + 1), :32] for dy in range(3)]
        tails.append(jnp.zeros_like(tails[0]))
        pieces[7 * other + 6, :out_rows] = jnp.concatenate(tails, axis=1).astype(BF)

    @pl.loop(0, ydim)
    def _(d):
        other = lax.rem(y + d, ydim)

        @pl.when((t != 6) | (d > 0))
        def _():
            send_piece(other, 6)

    for half in range(2):
        for h in range(2):
            rows = [lat_dense[16 * half + 8 * h + i] for i in range(8)]
            for i, row in enumerate(swap_blocks(rows, lane)):
                lat_tiles[8 * half + i, :, 128 * h : 128 * h + 128] = row.astype(BF)
    for k in range(12):
        held = lat_tiles[tiles_ref[0, k]]
        lat_ref[k] = jnp.where(k < count, held, jnp.zeros_like(held))

    owner = t < 7

    @pl.when(owner)
    def _():
        parts[spot] = pieces[7 * y + t]
        arrived(parts.at[pl.ds(0, plane - 1)], piece_recv)
        total = parts[0].astype(F32)
        for i in range(1, plane):
            total = total + parts[i].astype(F32)
        z_in[b] = total.astype(BF)
        for d in sorted(range(1, zdim), key=lambda d: -min(d, zdim - d)):
            remote(z_in.at[b], z_in.at[b], z_send.at[d], z_recv, tile=lax.rem(b + d, zdim)).start()
        arrived(z_in.at[pl.ds(0, zdim - 1)], z_recv)
        total = z_in[0].astype(F32)
        for i in range(1, zdim):
            total = total + z_in[i].astype(F32)
        final[t] = total[:out_rows]
        for d in range(1, tdim):
            remote(
                final.at[t], final.at[t], final_send.at[d - 1], final_recv.at[t], tm=lax.rem(t + d, tdim)
            ).start()

    for l in range(7):
        @pl.when(t != l)
        def _():
            arrived(final.at[l], final_recv.at[l])

    for dy in range(3):
        grad_ref[:, 288 * dy : 288 * (dy + 1)] = jnp.concatenate(
            [final[2 * dy], final[2 * dy + 1], final[6][:, 32 * dy : 32 * (dy + 1)]], axis=1
        )

    for cond, make in pend:
        @pl.when(cond)
        def _(make=make):
            make().wait_send()

    @pl.loop(0, tdim - 1)
    def _(f):
        @pl.when(t != f + 1)
        def _():
            arrived(ctx_out.at[f], ctx_send.at[f])

        @pl.when((t == 0) | (t == tdim - 1))
        def _():
            arrived(ctx_out.at[f, 0], ctx_edge_send.at[f])

    @pl.when(owner)
    def _():
        arrived(pieces.at[pl.ds(0, 7 * ydim - 1)], piece_send)
        for d in range(1, zdim):
            arrived(z_in.at[b], z_send.at[d])
        for d in range(1, tdim):
            arrived(final.at[t], final_send.at[d - 1])

    @pl.when(t == tdim - 1)
    def _():
        arrived(pieces, piece_send)


def body(sizes, frames_in, w_in, gate_bias, w_ent, active_tiles, active_count, cotangent):
    ydim, tdim, zdim = sizes
    plane = ydim * tdim
    per = 32 // tdim
    out_rows = 96 // ydim
    held_rows = -(-out_rows // 16) * 16
    vmem = pl.BlockSpec(memory_space=pltpu.VMEM)
    hbm = pl.BlockSpec(memory_space=pltpu.HBM)
    dma = pltpu.SemaphoreType.DMA
    latent, grad = pl.pallas_call(
        functools.partial(kernel, sizes),
        out_shape=(
            jax.ShapeDtypeStruct((12, 48, 256), BF),
            jax.ShapeDtypeStruct((out_rows, 864), F32),
        ),
        in_specs=[hbm] * 7,
        out_specs=(vmem, vmem),
        scratch_shapes=[
            pltpu.VMEM((96, 432), BF),
            pltpu.VMEM((1, 48), F32),
            pltpu.VMEM((96, 864), BF),
            pltpu.SMEM((1, 12), jnp.int32),
            pltpu.SMEM((1, 1, 1), jnp.int32),
            pltpu.VMEM((48, 32, 128), BF),
            pltpu.VMEM((48 * 32, 128), F32),
            pltpu.VMEM((34, 48, 128), BF),
            pltpu.VMEM((12, 48, 256), BF),
            pltpu.VMEM((tdim, per + 2, 48, 128), BF),
            pltpu.VMEM((tdim, 48, 128), BF),
            pltpu.VMEM((2, 48, 128), BF),
            pltpu.VMEM(((per + 2) * 144, 128), BF),
            pltpu.VMEM((tdim - 1, 48, per * 128), F32),
            pltpu.VMEM((tdim - 1, 48, per * 128), F32),
            pltpu.VMEM((48, per * 128), F32),
            pltpu.VMEM((tdim - 1, per, 48, 128), BF),
            pltpu.VMEM((34, 48, 128), BF),
            pltpu.VMEM((2, 48, 128), BF),
            pltpu.VMEM((2, 96, 432), BF),
            pltpu.VMEM((2, 96, 2048), F32),
            pltpu.VMEM((34 * 288, 128), BF),
            pltpu.VMEM((32, 48, 128), F32),
            pltpu.VMEM((36 * 96, 128), BF),
            pltpu.VMEM((32, 48, 128), F32),
            pltpu.VMEM((16, 48, 256), BF),
            pltpu.VMEM((288, 256), F32),
            pltpu.VMEM((7 * ydim, held_rows, 128), BF),
            pltpu.VMEM((plane, held_rows, 128), BF),
            pltpu.VMEM((zdim, held_rows, 128), BF),
            pltpu.VMEM((7, out_rows, 128), F32),
            dma((7,)),
            dma((tdim,)), dma((tdim,)),
            dma((2,)), dma((tdim,)),
            dma((2,)), dma((2,)),
            dma((tdim - 1,)), dma((tdim,)),
            dma((tdim - 1,)), dma((2,)),
            dma, dma,
            dma((zdim,)), dma,
            dma((tdim - 1,)), dma((7,)),
            pltpu.SemaphoreType.REGULAR((len(relay_strides(zdim)) + 1,)),
        ],
        compiler_params=pltpu.CompilerParams(
            collective_id=0, has_side_effects=True, vmem_limit_bytes=32 * 1024 * 1024
        ),
        cost_estimate=pl.CostEstimate(flops=1_700_000_000, bytes_accessed=1_500_000, transcendentals=1_500_000),
        name="coding_window",
    )(
        pltpu.with_memory_space_constraint(frames_in[0, 0], pltpu.HBM),
        pltpu.with_memory_space_constraint(w_in, pltpu.HBM),
        pltpu.with_memory_space_constraint(gate_bias[None], pltpu.HBM),
        pltpu.with_memory_space_constraint(w_ent, pltpu.HBM),
        pltpu.with_memory_space_constraint(active_tiles[0, 0], pltpu.HBM),
        active_count,
        pltpu.with_memory_space_constraint(cotangent[0, 0, 0], pltpu.HBM),
    )
    return (latent[None, None, None], grad)


def solution(mesh):
    sizes = tuple(mesh.shape[axis] for axis in ("dp", "tm", "tile"))
    return jax.shard_map(
        functools.partial(body, sizes),
        mesh=mesh,
        in_specs=(
            P("dp", "tm", None, "tile", None),
            P(),
            P(),
            P(),
            P("dp", "tm", "tile", None),
            P("dp", "tm", "tile"),
            P("dp", "tm", "tile", None, None, None),
        ),
        out_specs=(P("dp", "tm", "tile", None, None, None), P("dp", None)),
        check_vma=False,
    )
```

```python
import functools

import jax
import jax.numpy as jnp
from jax import lax
from jax.experimental import pallas as pl
from jax.experimental.pallas import tpu as pltpu
from jax.sharding import PartitionSpec as P

BF = jnp.bfloat16
F32 = jnp.float32
MESH = pl.DeviceIdType.MESH


NEAR = 2


def relay_strides(size):
    strides, known = [], NEAR
    while known < size // 2:
        strides.append(known)
        known *= 2
    return strides


def swap_blocks(parts, lane):
    for m in (1, 2, 4):
        low = (lane & (16 * m)) == 0
        done = list(parts)
        for p in range(8):
            if p & m:
                continue
            q = p | m
            done[p] = jnp.where(low, parts[p], pltpu.roll(parts[q], 16 * m, 1))
            done[q] = jnp.where(low, pltpu.roll(parts[p], 128 - 16 * m, 1), parts[q])
        parts = done
    return parts


def store_shifts(out_ref, start, gap, value, lane):
    wide = value.astype(F32)
    before = jnp.where(lane == 0, 0.0, pltpu.roll(wide, 1, 1))
    after = jnp.where(lane == 127, 0.0, pltpu.roll(wide, 127, 1))
    out_ref[pl.ds(start, 48), :] = before.astype(BF)
    out_ref[pl.ds(start + gap, 48), :] = value
    out_ref[pl.ds(start + 2 * gap, 48), :] = after.astype(BF)


def kernel(
    sizes,
    x_hbm, w_in_hbm, bias_hbm, w_ent_hbm, tiles_hbm, count_hbm, cot_hbm,
    lat_ref, grad_ref,
    w_in_ref, bias_ref, w_ent_ref, tiles_ref, count_ref,
    xv, xf, xb, cotv, frame_rows, edge_rows, halo, conv_in, gates, drives, state, ctx_out, ctx, ctx_edge,
    w_part, pre_x, joined, cot_dense, push, lat_dense, lat_tiles, grad_all, pieces, parts, z_in, final,
    load_sem, main_send, main_recv, edge_send, edge_recv, halo_send, halo_recv,
    ctx_send, ctx_recv, ctx_edge_send, ctx_edge_recv,
    piece_send, piece_recv, z_send, z_recv, final_send, final_recv, relay_sem,
):
    ydim, tdim, zdim = sizes
    y = lax.axis_index("dp")
    t = lax.axis_index("tm")
    b = lax.axis_index("tile")
    above = lax.rem(b + zdim - 1, zdim)
    below = lax.rem(b + 1, zdim)
    plane = ydim * tdim
    spot = y * tdim + t
    per = 32 // tdim
    strides = relay_strides(zdim)
    out_rows = 96 // ydim
    pend = []

    def send(cond, make):
        @pl.when(cond)
        def _():
            make().start()

        pend.append((cond, make))

    def remote(src, dst, ssem, rsem, **where):
        return pltpu.make_async_remote_copy(
            src_ref=src, dst_ref=dst, send_sem=ssem, recv_sem=rsem, device_id=where, device_id_type=MESH
        )

    def arrived(ref, sem):
        pltpu.make_async_copy(ref, ref, sem).wait()

    loads = [
        pltpu.make_async_copy(src, dst, load_sem.at[i])
        for i, (src, dst) in enumerate(
            (
                (x_hbm, xv), (tiles_hbm, tiles_ref), (count_hbm, count_ref), (cot_hbm, cotv),
                (w_in_hbm, w_in_ref), (bias_hbm, bias_ref), (w_ent_hbm, w_ent_ref),
            )
        )
    ]
    for load in loads:
        load.start()

    barrier = pltpu.get_barrier_semaphore()

    greeted = 0
    for axis, size, offsets in (
        ("tm", tdim, range(1, tdim)),
        ("tile", zdim, [d for d in range(1, zdim) if min(d, zdim - d) <= NEAR]),
        ("dp", ydim, range(1, ydim)),
    ):
        for d in offsets:
            peer = lax.rem(lax.axis_index(axis) + d, size)
            pl.semaphore_signal(barrier, inc=1, device_id={axis: peer}, device_id_type=MESH)
            greeted += 1

    lane = lax.broadcasted_iota(jnp.int32, (48, 128), 1)
    blank = jnp.zeros((48, 128), BF)

    loads[0].wait()
    xf[...] = xv[...].astype(F32).reshape(48 * 32, 128)
    xb[0] = blank
    xb[33] = blank
    for r in range(32):
        xb[1 + r] = xf[pl.ds(r, 48, stride=32), :].astype(BF)

    pl.semaphore_wait(barrier, greeted)

    def relay(step, axis, size, offsets):
        for d in offsets:
            peer = lax.rem(lax.axis_index(axis) + d, size)
            pl.semaphore_signal(relay_sem.at[step], inc=1, device_id={axis: peer}, device_id_type=MESH)

    sends = t < tdim - 1
    always = t >= 0
    send(always, lambda: remote(xb.at[32], halo.at[0], halo_send.at[0], halo_recv.at[0], tile=below))
    send(always, lambda: remote(xb.at[1], halo.at[1], halo_send.at[1], halo_recv.at[1], tile=above))
    for d in range(1, tdim):
        j = lax.rem(t + tdim - d, tdim)
        send(
            sends,
            lambda d=d, j=j: remote(
                xb.at[pl.ds(per * j, per + 2)], frame_rows.at[t], main_send.at[d], main_recv.at[t], tm=j
            ),
        )
    relay(len(strides), "dp", ydim, range(1, ydim))
    if strides:
        relay(0, "tile", zdim, (strides[0], zdim - strides[0]))

    @pl.when(sends)
    def _():
        frame_rows[t] = xb[pl.ds(per * t, per + 2)]

    for r in range(1, 33):
        store_shifts(joined, 288 * r, 96, xb[r], lane)

    for load in loads[1:4]:
        load.wait()
    count = count_ref[0, 0, 0]
    slots = []
    for n in range(16):
        found = jnp.int32(0)
        for k in range(12):
            found = jnp.where((tiles_ref[0, k] == n) & (k < count), k + 1, found)
        slots.append(found)
    for half in range(2):
        for h in range(2):
            columns = slice(128 * h, 128 * h + 128)
            rows = []
            for i in range(8):
                found = slots[8 * half + i]
                held = cotv[jnp.maximum(found - 1, 0), :, columns].astype(F32)
                rows.append(jnp.where(found > 0, held, 0.0))
            for i, row in enumerate(swap_blocks(rows, lane)):
                cot_dense[16 * half + 8 * h + i] = row

    for edge, row, there in ((0, 0, b > 0), (1, 33, b < zdim - 1)):
        arrived(halo.at[edge], halo_recv.at[edge])
        end = edge * (tdim - 1)
        send(
            sends & (t != end),
            lambda edge=edge, end=end: remote(
                halo.at[edge], edge_rows.at[t], edge_send.at[edge], edge_recv.at[t], tm=end
            ),
        )
        store_shifts(joined, 288 * row, 96, jnp.where(there, halo[edge], blank), lane)

    @pl.when(t == 0)
    def _():
        edge_rows[0] = halo[0]

    loads[6].wait()
    w_all = w_ent_ref[...]
    for part in range(2):
        w_part[part] = jnp.concatenate([w_all[:, 96 * k + 48 * part : 96 * k + 48 * part + 48] for k in range(9)], axis=1)

    def taps(part, r):
        starts = [288 * (r + dy) + 96 * dx + 48 * part for dy in range(3) for dx in range(3)]
        return jnp.concatenate([joined[start : start + 48, :] for start in starts], axis=0)

    for block in range(2):
        cells = jnp.concatenate([taps(0, 16 * block + r) for r in range(16)], axis=1)
        pre_x[block] = jnp.dot(w_part[0], cells, preferred_element_type=F32)

    for step in range(1, len(strides)):
        pl.semaphore_wait(relay_sem.at[step - 1], 2)
        relay(step, "tile", zdim, (strides[step], zdim - strides[step]))

    state[...] = jnp.zeros_like(state)
    for load in loads[4:6]:
        load.wait()
    bias = bias_ref[...].T[:48, :1]

    def convolve(f):
        @pl.when(t != f)
        def _():
            arrived(frame_rows.at[f], main_recv.at[f])

        for end, row, there in ((0, 0, b > 0), (tdim - 1, per + 1, b < zdim - 1)):
            @pl.when(t == end)
            def _():
                @pl.when(f != end)
                def _():
                    arrived(edge_rows.at[f], edge_recv.at[f])

                frame_rows[f, row] = jnp.where(there, edge_rows[f], blank)

        for r in range(per + 2):
            store_shifts(conv_in, 144 * r, 48, frame_rows[f, r], lane)
        cells = jnp.concatenate([conv_in[pl.ds(144 * r, 432), :] for r in range(per)], axis=1)
        mixed = jnp.dot(w_in_ref[...], cells, preferred_element_type=F32)
        gates[f] = 0.5 * jnp.tanh(0.5 * (mixed[:48] + bias)) + 0.5
        drives[f] = jnp.tanh(mixed[48:])

    def advance(f):
        now = gates[f] * state[...] + drives[f]
        state[...] = now
        for r in range(per):
            ctx_out[f, r] = now[:, 128 * r : 128 * r + 128].astype(BF)

        @pl.when(t != f + 1)
        def _():
            remote(
                ctx_out.at[f], ctx.at[pl.ds(1 + per * t, per)], ctx_send.at[f], ctx_recv.at[t], tm=f + 1
            ).start()

        @pl.when(t == f + 1)
        def _():
            ctx[pl.ds(1 + per * t, per)] = ctx_out[f]

        @pl.when(t == tdim - 1)
        def _():
            remote(
                ctx_out.at[f, per - 1], ctx_edge.at[0], ctx_edge_send.at[f], ctx_edge_recv.at[0],
                tm=f + 1, tile=below,
            ).start()

        @pl.when(t == 0)
        def _():
            remote(
                ctx_out.at[f, 0], ctx_edge.at[1], ctx_edge_send.at[f], ctx_edge_recv.at[1],
                tm=f + 1, tile=above,
            ).start()

    @pl.loop(0, tdim)
    def _(i):
        f = lax.rem(t + i, tdim)

        @pl.when(f < tdim - 1)
        def _():
            convolve(f)

            @pl.when((f < t) | (t == 0))
            def _():
                advance(f)

    @pl.loop(0, tdim - 1)
    def _(f):
        @pl.when((f >= t) & (t > 0))
        def _():
            advance(f)

    if strides:
        pl.semaphore_wait(relay_sem.at[len(strides) - 1], 2)
    if ydim > 1:
        pl.semaphore_wait(relay_sem.at[len(strides)], ydim - 1)

    @pl.when(t == 0)
    def _():
        ctx[...] = jnp.zeros_like(ctx)
        ctx_edge[...] = jnp.zeros_like(ctx_edge)

    for j in range(tdim):
        @pl.when((t > 0) & (t != j))
        def _():
            arrived(ctx.at[pl.ds(1 + per * j, per)], ctx_recv.at[j])

        for r in range(1 + per * j, 1 + per * (j + 1)):
            store_shifts(joined, 288 * r + 48, 96, ctx[r], lane)

    for edge, row, there in ((0, 0, b > 0), (1, 33, b < zdim - 1)):
        @pl.when(t > 0)
        def _():
            arrived(ctx_edge.at[edge], ctx_edge_recv.at[edge])

        store_shifts(joined, 288 * row + 48, 96, jnp.where(there, ctx_edge[edge], blank), lane)

    for r in (-2, -1, 32, 33):
        push[96 * (33 - r) : 96 * (34 - r), :] = jnp.zeros((96, 128), BF)
    for block in range(2):
        cells = jnp.concatenate([taps(1, 16 * block + r) for r in range(16)], axis=1)
        pre = pre_x[block] + jnp.dot(w_part[1], cells, preferred_element_type=F32)
        for i in range(16):
            r = 16 * block + i
            mean = pre[:48, 128 * i : 128 * i + 128]
            spread = pre[48:, 128 * i : 128 * i + 128]
            small = jnp.exp(-jnp.abs(spread))
            sigma = 0.5 + jnp.maximum(spread, 0.0) + jnp.log(1.0 + small)
            slope = jnp.where(spread >= 0, 1.0, small) / (1.0 + small)
            scale = 1.0 / sigma
            lat = (xb[r + 1].astype(F32) - mean) * scale
            lat_dense[r] = lat
            near = -cot_dense[r] * scale
            push[96 * (33 - r) : 96 * (33 - r) + 48, :] = near.astype(BF)
            push[96 * (33 - r) + 48 : 96 * (34 - r), :] = (near * lat * slope).astype(BF)

    near = jnp.concatenate([push[96 * (33 - r) : 96 * (36 - r), :] for r in range(34)], axis=1)

    def gradient(first, last):
        rows = jnp.concatenate([joined[288 * r + first : 288 * r + last, :] for r in range(34)], axis=1)
        return lax.dot_general(near, rows, (((1,), (1,)), ((), ())), preferred_element_type=F32)

    def send_piece(other, l):
        remote(pieces.at[7 * other + l], parts.at[spot], piece_send, piece_recv, dp=other, tm=l).start()

    grad_all[...] = gradient(0, 256)
    for other in range(ydim):
        for dy in range(3):
            block = grad_all[96 * dy + out_rows * other : 96 * dy + out_rows * (other + 1), :]
            pieces[7 * other + 2 * dy, :out_rows] = block[:, :128].astype(BF)
            pieces[7 * other + 2 * dy + 1, :out_rows] = block[:, 128:].astype(BF)

    def hops(way):
        dy, dt = way
        return min(dy, ydim - dy) + min(dt // 2, (tdim - dt) // 2)

    ways = [(dy, dt) for dy in range(ydim) for dt in range(tdim) if dy + dt > 0]
    for dy, dt in sorted(ways, key=hops, reverse=True):
        l = lax.rem(t + dt, tdim)

        @pl.when(l < 6)
        def _(dy=dy, l=l):
            send_piece(lax.rem(y + dy, ydim), l)

    grad_all[:, :32] = gradient(256, 288)
    for other in range(ydim):
        tails = [grad_all[96 * dy + out_rows * other : 96 * dy + out_rows * (other + 1), :32] for dy in range(3)]
        tails.append(jnp.zeros_like(tails[0]))
        pieces[7 * other + 6, :out_rows] = jnp.concatenate(tails, axis=1).astype(BF)

    @pl.loop(0, ydim)
    def _(d):
        other = lax.rem(y + d, ydim)

        @pl.when((t != 6) | (d > 0))
        def _():
            send_piece(other, 6)

    for half in range(2):
        for h in range(2):
            rows = [lat_dense[16 * half + 8 * h + i] for i in range(8)]
            for i, row in enumerate(swap_blocks(rows, lane)):
                lat_tiles[8 * half + i, :, 128 * h : 128 * h + 128] = row.astype(BF)
    for k in range(12):
        held = lat_tiles[tiles_ref[0, k]]
        lat_ref[k] = jnp.where(k < count, held, jnp.zeros_like(held))

    owner = t < 7

    for cond, make in pend:
        @pl.when(cond)
        def _(make=make):
            make().wait_send()

    @pl.loop(0, tdim - 1)
    def _(f):
        @pl.when(t != f + 1)
        def _():
            arrived(ctx_out.at[f], ctx_send.at[f])

        @pl.when((t == 0) | (t == tdim - 1))
        def _():
            arrived(ctx_out.at[f, 0], ctx_edge_send.at[f])

    @pl.when(owner)
    def _():
        parts[spot] = pieces[7 * y + t]
        arrived(parts.at[pl.ds(0, plane - 1)], piece_recv)
        total = parts[0].astype(F32)
        for i in range(1, plane):
            total = total + parts[i].astype(F32)
        z_in[b] = total.astype(BF)
        for d in sorted(range(1, zdim), key=lambda d: -min(d, zdim - d)):
            remote(z_in.at[b], z_in.at[b], z_send.at[d], z_recv, tile=lax.rem(b + d, zdim)).start()
        arrived(z_in.at[pl.ds(0, zdim - 1)], z_recv)
        total = z_in[0].astype(F32)
        for i in range(1, zdim):
            total = total + z_in[i].astype(F32)
        final[t] = total[:out_rows]
        for d in range(1, tdim):
            remote(
                final.at[t], final.at[t], final_send.at[d - 1], final_recv.at[t], tm=lax.rem(t + d, tdim)
            ).start()

    @pl.when(owner)
    def _():
        arrived(pieces.at[pl.ds(0, 7 * ydim - 1)], piece_send)
        for d in range(1, zdim):
            arrived(z_in.at[b], z_send.at[d])

    @pl.when(t == tdim - 1)
    def _():
        arrived(pieces, piece_send)

    for l in range(7):
        @pl.when(t != l)
        def _():
            arrived(final.at[l], final_recv.at[l])

    for dy in range(3):
        grad_ref[:, 288 * dy : 288 * (dy + 1)] = jnp.concatenate(
            [final[2 * dy], final[2 * dy + 1], final[6][:, 32 * dy : 32 * (dy + 1)]], axis=1
        )

    @pl.when(owner)
    def _():
        for d in range(1, tdim):
            arrived(final.at[t], final_send.at[d - 1])


def store_kernel(lat_ref, grad_ref, lat_hbm, grad_hbm, sem):
    copies = [
        pltpu.make_async_copy(lat_ref, lat_hbm, sem.at[0]),
        pltpu.make_async_copy(grad_ref, grad_hbm, sem.at[1]),
    ]
    for copy in copies:
        copy.start()
    for copy in copies:
        copy.wait()


def body(sizes, frames_in, w_in, gate_bias, w_ent, active_tiles, active_count, cotangent):
    ydim, tdim, zdim = sizes
    plane = ydim * tdim
    per = 32 // tdim
    out_rows = 96 // ydim
    held_rows = -(-out_rows // 16) * 16
    vmem = pl.BlockSpec(memory_space=pltpu.VMEM)
    hbm = pl.BlockSpec(memory_space=pltpu.HBM)
    dma = pltpu.SemaphoreType.DMA
    latent, grad = pl.pallas_call(
        functools.partial(kernel, sizes),
        out_shape=(
            jax.ShapeDtypeStruct((12, 48, 256), BF),
            jax.ShapeDtypeStruct((out_rows, 864), F32),
        ),
        in_specs=[hbm] * 7,
        out_specs=(vmem, vmem),
        scratch_shapes=[
            pltpu.VMEM((96, 432), BF),
            pltpu.VMEM((1, 48), F32),
            pltpu.VMEM((96, 864), BF),
            pltpu.SMEM((1, 12), jnp.int32),
            pltpu.SMEM((1, 1, 1), jnp.int32),
            pltpu.VMEM((48, 32, 128), BF),
            pltpu.VMEM((48 * 32, 128), F32),
            pltpu.VMEM((34, 48, 128), BF),
            pltpu.VMEM((12, 48, 256), BF),
            pltpu.VMEM((tdim, per + 2, 48, 128), BF),
            pltpu.VMEM((tdim, 48, 128), BF),
            pltpu.VMEM((2, 48, 128), BF),
            pltpu.VMEM(((per + 2) * 144, 128), BF),
            pltpu.VMEM((tdim - 1, 48, per * 128), F32),
            pltpu.VMEM((tdim - 1, 48, per * 128), F32),
            pltpu.VMEM((48, per * 128), F32),
            pltpu.VMEM((tdim - 1, per, 48, 128), BF),
            pltpu.VMEM((34, 48, 128), BF),
            pltpu.VMEM((2, 48, 128), BF),
            pltpu.VMEM((2, 96, 432), BF),
            pltpu.VMEM((2, 96, 2048), F32),
            pltpu.VMEM((34 * 288, 128), BF),
            pltpu.VMEM((32, 48, 128), F32),
            pltpu.VMEM((36 * 96, 128), BF),
            pltpu.VMEM((32, 48, 128), F32),
            pltpu.VMEM((16, 48, 256), BF),
            pltpu.VMEM((288, 256), F32),
            pltpu.VMEM((7 * ydim, held_rows, 128), BF),
            pltpu.VMEM((plane, held_rows, 128), BF),
            pltpu.VMEM((zdim, held_rows, 128), BF),
            pltpu.VMEM((7, out_rows, 128), F32),
            dma((7,)),
            dma((tdim,)), dma((tdim,)),
            dma((2,)), dma((tdim,)),
            dma((2,)), dma((2,)),
            dma((tdim - 1,)), dma((tdim,)),
            dma((tdim - 1,)), dma((2,)),
            dma, dma,
            dma((zdim,)), dma,
            dma((tdim - 1,)), dma((7,)),
            pltpu.SemaphoreType.REGULAR((len(relay_strides(zdim)) + 1,)),
        ],
        compiler_params=pltpu.CompilerParams(
            collective_id=0, has_side_effects=True, vmem_limit_bytes=32 * 1024 * 1024
        ),
        cost_estimate=pl.CostEstimate(flops=1_700_000_000, bytes_accessed=1_500_000, transcendentals=1_500_000),
        name="coding_window",
    )(
        pltpu.with_memory_space_constraint(frames_in[0, 0], pltpu.HBM),
        pltpu.with_memory_space_constraint(w_in, pltpu.HBM),
        pltpu.with_memory_space_constraint(gate_bias[None], pltpu.HBM),
        pltpu.with_memory_space_constraint(w_ent, pltpu.HBM),
        pltpu.with_memory_space_constraint(active_tiles[0, 0], pltpu.HBM),
        active_count,
        pltpu.with_memory_space_constraint(cotangent[0, 0, 0], pltpu.HBM),
    )
    anywhere = pl.BlockSpec(memory_space=pl.ANY)
    latent, grad = pl.pallas_call(
        store_kernel,
        out_shape=(
            jax.ShapeDtypeStruct((12, 48, 256), BF),
            jax.ShapeDtypeStruct((out_rows, 864), F32),
        ),
        in_specs=[anywhere] * 2,
        out_specs=(anywhere,) * 2,
        scratch_shapes=[dma((2,))],
        cost_estimate=pl.CostEstimate(flops=0, bytes_accessed=800_000, transcendentals=0),
        name="store_outputs",
    )(latent, grad)
    return (latent[None, None, None], grad)


def solution(mesh):
    sizes = tuple(mesh.shape[axis] for axis in ("dp", "tm", "tile"))
    return jax.shard_map(
        functools.partial(body, sizes),
        mesh=mesh,
        in_specs=(
            P("dp", "tm", None, "tile", None),
            P(),
            P(),
            P(),
            P("dp", "tm", "tile", None),
            P("dp", "tm", "tile"),
            P("dp", "tm", "tile", None, None, None),
        ),
        out_specs=(P("dp", "tm", "tile", None, None, None), P("dp", None)),
        check_vma=False,
    )
```

```python
import functools

import jax
import jax.numpy as jnp
from jax import lax
from jax.experimental import pallas as pl
from jax.experimental.pallas import tpu as pltpu
from jax.sharding import PartitionSpec as P

BF = jnp.bfloat16
F32 = jnp.float32
MESH = pl.DeviceIdType.MESH


NEAR = 2


def relay_strides(size):
    strides, known = [], NEAR
    while known < size // 2:
        strides.append(known)
        known *= 2
    return strides


def shares(out_rows):
    first, last = 6 * out_rows // 16, -(-out_rows // 16)
    return [16 * (first * (i + 1) // 6 - first * i // 6) for i in range(6)] + [
        16 * (last * (i + 1) // 2 - last * i // 2) for i in range(2)
    ]


def swap_blocks(parts, lane):
    for m in (1, 2, 4):
        low = (lane & (16 * m)) == 0
        done = list(parts)
        for p in range(8):
            if p & m:
                continue
            q = p | m
            done[p] = jnp.where(low, parts[p], pltpu.roll(parts[q], 16 * m, 1))
            done[q] = jnp.where(low, pltpu.roll(parts[p], 128 - 16 * m, 1), parts[q])
        parts = done
    return parts


def store_shifts(out_ref, start, gap, value, lane):
    wide = value.astype(F32)
    before = jnp.where(lane == 0, 0.0, pltpu.roll(wide, 1, 1))
    after = jnp.where(lane == 127, 0.0, pltpu.roll(wide, 127, 1))
    out_ref[pl.ds(start, 48), :] = before.astype(BF)
    out_ref[pl.ds(start + gap, 48), :] = value
    out_ref[pl.ds(start + 2 * gap, 48), :] = after.astype(BF)


def kernel(
    sizes,
    x_hbm, w_in_hbm, bias_hbm, w_ent_hbm, tiles_hbm, count_hbm, cot_hbm,
    lat_ref, grad_ref,
    w_in_ref, bias_ref, w_ent_ref, tiles_ref, count_ref,
    xv, xf, xb, cotv, frame_rows, edge_rows, halo, conv_in, gates, drives, state, ctx_out, ctx, ctx_edge,
    w_part, pre_x, joined, cot_dense, push, lat_dense, lat_tiles, grad_all, pieces, parts, z_in, final,
    load_sem, main_send, main_recv, edge_send, edge_recv, halo_send, halo_recv,
    ctx_send, ctx_recv, ctx_edge_send, ctx_edge_recv,
    piece_send, piece_recv, z_send, z_recv, final_send, final_recv, relay_sem,
):
    ydim, tdim, zdim = sizes
    y = lax.axis_index("dp")
    t = lax.axis_index("tm")
    b = lax.axis_index("tile")
    above = lax.rem(b + zdim - 1, zdim)
    below = lax.rem(b + 1, zdim)
    plane = ydim * tdim
    spot = y * tdim + t
    per = 32 // tdim
    strides = relay_strides(zdim)
    out_rows = 96 // ydim
    shared = shares(out_rows)
    block_rows = sum(shared)
    pend = []

    def send(cond, make):
        @pl.when(cond)
        def _():
            make().start()

        pend.append((cond, make))

    def remote(src, dst, ssem, rsem, **where):
        return pltpu.make_async_remote_copy(
            src_ref=src, dst_ref=dst, send_sem=ssem, recv_sem=rsem, device_id=where, device_id_type=MESH
        )

    def arrived(ref, sem):
        pltpu.make_async_copy(ref, ref, sem).wait()

    loads = [
        pltpu.make_async_copy(src, dst, load_sem.at[i])
        for i, (src, dst) in enumerate(
            (
                (x_hbm, xv), (tiles_hbm, tiles_ref), (count_hbm, count_ref), (cot_hbm, cotv),
                (w_in_hbm, w_in_ref), (bias_hbm, bias_ref), (w_ent_hbm, w_ent_ref),
            )
        )
    ]
    for load in loads:
        load.start()

    barrier = pltpu.get_barrier_semaphore()

    greeted = 0
    for axis, size, offsets in (
        ("tm", tdim, range(1, tdim)),
        ("tile", zdim, [d for d in range(1, zdim) if min(d, zdim - d) <= NEAR]),
        ("dp", ydim, range(1, ydim)),
    ):
        for d in offsets:
            peer = lax.rem(lax.axis_index(axis) + d, size)
            pl.semaphore_signal(barrier, inc=1, device_id={axis: peer}, device_id_type=MESH)
            greeted += 1

    lane = lax.broadcasted_iota(jnp.int32, (48, 128), 1)
    blank = jnp.zeros((48, 128), BF)

    loads[0].wait()
    xf[...] = xv[...].astype(F32).reshape(48 * 32, 128)
    xb[0] = blank
    xb[33] = blank
    for r in range(32):
        xb[1 + r] = xf[pl.ds(r, 48, stride=32), :].astype(BF)

    pl.semaphore_wait(barrier, greeted)

    def relay(step, axis, size, offsets):
        for d in offsets:
            peer = lax.rem(lax.axis_index(axis) + d, size)
            pl.semaphore_signal(relay_sem.at[step], inc=1, device_id={axis: peer}, device_id_type=MESH)

    sends = t < tdim - 1
    always = t >= 0
    send(always, lambda: remote(xb.at[32], halo.at[0], halo_send.at[0], halo_recv.at[0], tile=below))
    send(always, lambda: remote(xb.at[1], halo.at[1], halo_send.at[1], halo_recv.at[1], tile=above))
    for d in range(1, tdim):
        j = lax.rem(t + tdim - d, tdim)
        send(
            sends,
            lambda d=d, j=j: remote(
                xb.at[pl.ds(per * j, per + 2)], frame_rows.at[t], main_send.at[d], main_recv.at[t], tm=j
            ),
        )
    relay(len(strides), "dp", ydim, range(1, ydim))
    if strides:
        relay(0, "tile", zdim, (strides[0], zdim - strides[0]))

    @pl.when(sends)
    def _():
        frame_rows[t] = xb[pl.ds(per * t, per + 2)]

    for r in range(1, 33):
        store_shifts(joined, 288 * r, 96, xb[r], lane)

    for load in loads[1:4]:
        load.wait()
    count = count_ref[0, 0, 0]
    slots = []
    for n in range(16):
        found = jnp.int32(0)
        for k in range(12):
            found = jnp.where((tiles_ref[0, k] == n) & (k < count), k + 1, found)
        slots.append(found)
    for half in range(2):
        for h in range(2):
            columns = slice(128 * h, 128 * h + 128)
            rows = []
            for i in range(8):
                found = slots[8 * half + i]
                held = cotv[jnp.maximum(found - 1, 0), :, columns].astype(F32)
                rows.append(jnp.where(found > 0, held, 0.0))
            for i, row in enumerate(swap_blocks(rows, lane)):
                cot_dense[16 * half + 8 * h + i] = row

    for edge, row, there in ((0, 0, b > 0), (1, 33, b < zdim - 1)):
        arrived(halo.at[edge], halo_recv.at[edge])
        end = edge * (tdim - 1)
        send(
            sends & (t != end),
            lambda edge=edge, end=end: remote(
                halo.at[edge], edge_rows.at[t], edge_send.at[edge], edge_recv.at[t], tm=end
            ),
        )
        store_shifts(joined, 288 * row, 96, jnp.where(there, halo[edge], blank), lane)

    @pl.when(t == 0)
    def _():
        edge_rows[0] = halo[0]

    loads[6].wait()
    w_all = w_ent_ref[...]
    for part in range(2):
        w_part[part] = jnp.concatenate([w_all[:, 96 * k + 48 * part : 96 * k + 48 * part + 48] for k in range(9)], axis=1)

    def taps(part, r):
        starts = [288 * (r + dy) + 96 * dx + 48 * part for dy in range(3) for dx in range(3)]
        return jnp.concatenate([joined[start : start + 48, :] for start in starts], axis=0)

    for block in range(2):
        cells = jnp.concatenate([taps(0, 16 * block + r) for r in range(16)], axis=1)
        pre_x[block] = jnp.dot(w_part[0], cells, preferred_element_type=F32)

    for step in range(1, len(strides)):
        pl.semaphore_wait(relay_sem.at[step - 1], 2)
        relay(step, "tile", zdim, (strides[step], zdim - strides[step]))

    state[...] = jnp.zeros_like(state)
    for load in loads[4:6]:
        load.wait()
    bias = bias_ref[...].T[:48, :1]

    def convolve(f):
        @pl.when(t != f)
        def _():
            arrived(frame_rows.at[f], main_recv.at[f])

        for end, row, there in ((0, 0, b > 0), (tdim - 1, per + 1, b < zdim - 1)):
            @pl.when(t == end)
            def _():
                @pl.when(f != end)
                def _():
                    arrived(edge_rows.at[f], edge_recv.at[f])

                frame_rows[f, row] = jnp.where(there, edge_rows[f], blank)

        for r in range(per + 2):
            store_shifts(conv_in, 144 * r, 48, frame_rows[f, r], lane)
        cells = jnp.concatenate([conv_in[pl.ds(144 * r, 432), :] for r in range(per)], axis=1)
        mixed = jnp.dot(w_in_ref[...], cells, preferred_element_type=F32)
        gates[f] = 0.5 * jnp.tanh(0.5 * (mixed[:48] + bias)) + 0.5
        drives[f] = jnp.tanh(mixed[48:])

    def advance(f):
        now = gates[f] * state[...] + drives[f]
        state[...] = now
        for r in range(per):
            ctx_out[f, r] = now[:, 128 * r : 128 * r + 128].astype(BF)

        @pl.when(t != f + 1)
        def _():
            remote(
                ctx_out.at[f], ctx.at[pl.ds(1 + per * t, per)], ctx_send.at[f], ctx_recv.at[t], tm=f + 1
            ).start()

        @pl.when(t == f + 1)
        def _():
            ctx[pl.ds(1 + per * t, per)] = ctx_out[f]

        @pl.when(t == tdim - 1)
        def _():
            remote(
                ctx_out.at[f, per - 1], ctx_edge.at[0], ctx_edge_send.at[f], ctx_edge_recv.at[0],
                tm=f + 1, tile=below,
            ).start()

        @pl.when(t == 0)
        def _():
            remote(
                ctx_out.at[f, 0], ctx_edge.at[1], ctx_edge_send.at[f], ctx_edge_recv.at[1],
                tm=f + 1, tile=above,
            ).start()

    @pl.loop(0, tdim)
    def _(i):
        f = lax.rem(t + i, tdim)

        @pl.when(f < tdim - 1)
        def _():
            convolve(f)

            @pl.when((f < t) | (t == 0))
            def _():
                advance(f)

    @pl.loop(0, tdim - 1)
    def _(f):
        @pl.when((f >= t) & (t > 0))
        def _():
            advance(f)

    if strides:
        pl.semaphore_wait(relay_sem.at[len(strides) - 1], 2)
    if ydim > 1:
        pl.semaphore_wait(relay_sem.at[len(strides)], ydim - 1)

    @pl.when(t == 0)
    def _():
        ctx[...] = jnp.zeros_like(ctx)
        ctx_edge[...] = jnp.zeros_like(ctx_edge)

    for j in range(tdim):
        @pl.when((t > 0) & (t != j))
        def _():
            arrived(ctx.at[pl.ds(1 + per * j, per)], ctx_recv.at[j])

        for r in range(1 + per * j, 1 + per * (j + 1)):
            store_shifts(joined, 288 * r + 48, 96, ctx[r], lane)

    for edge, row, there in ((0, 0, b > 0), (1, 33, b < zdim - 1)):
        @pl.when(t > 0)
        def _():
            arrived(ctx_edge.at[edge], ctx_edge_recv.at[edge])

        store_shifts(joined, 288 * row + 48, 96, jnp.where(there, ctx_edge[edge], blank), lane)

    for r in (-2, -1, 32, 33):
        push[96 * (33 - r) : 96 * (34 - r), :] = jnp.zeros((96, 128), BF)
    for block in range(2):
        cells = jnp.concatenate([taps(1, 16 * block + r) for r in range(16)], axis=1)
        pre = pre_x[block] + jnp.dot(w_part[1], cells, preferred_element_type=F32)
        for i in range(16):
            r = 16 * block + i
            mean = pre[:48, 128 * i : 128 * i + 128]
            spread = pre[48:, 128 * i : 128 * i + 128]
            small = jnp.exp(-jnp.abs(spread))
            sigma = 0.5 + jnp.maximum(spread, 0.0) + jnp.log(1.0 + small)
            slope = jnp.where(spread >= 0, 1.0, small) / (1.0 + small)
            scale = 1.0 / sigma
            lat = (xb[r + 1].astype(F32) - mean) * scale
            lat_dense[r] = lat
            near = -cot_dense[r] * scale
            push[96 * (33 - r) : 96 * (33 - r) + 48, :] = near.astype(BF)
            push[96 * (33 - r) + 48 : 96 * (34 - r), :] = (near * lat * slope).astype(BF)

    near = jnp.concatenate([push[96 * (33 - r) : 96 * (36 - r), :] for r in range(34)], axis=1)

    def gradient(first, last):
        rows = jnp.concatenate([joined[288 * r + first : 288 * r + last, :] for r in range(34)], axis=1)
        return lax.dot_general(near, rows, (((1,), (1,)), ((), ())), preferred_element_type=F32)

    def owned_from(l):
        return pl.multiple_of(sum(shared[k] * ((l + 7 - k) // 8) for k in range(7)), 16)

    def sized(l, among):
        for size in sorted({shared[k] for k in among}):
            has = l < 0
            for k in among:
                if shared[k] == size:
                    has = has | (l == k)
            yield size, has

    def send_piece(other, l, size):
        src = pieces.at[pl.ds(block_rows * other + owned_from(l), size)]
        remote(src, parts.at[spot, pl.ds(0, size)], piece_send, piece_recv, dp=other, tm=l).start()

    def hops(way):
        dy, dt = way
        return min(dy, ydim - dy) + min(dt // 2, (tdim - dt) // 2)

    ways = [(dy, dt) for dy in range(ydim) for dt in range(tdim) if dy + dt > 0]
    ways = sorted(ways, key=hops, reverse=True)

    def send_pieces(among):
        for dy, dt in ways:
            l = lax.rem(t + dt, tdim)
            for size, has in sized(l, among):
                @pl.when(has)
                def _(dy=dy, l=l, size=size):
                    send_piece(lax.rem(y + dy, ydim), l, size)

    grad_all[...] = gradient(0, 256)
    for other in range(ydim):
        for dy in range(3):
            block = grad_all[96 * dy + out_rows * other : 96 * dy + out_rows * (other + 1), :]
            for half in range(2):
                start = block_rows * other + out_rows * (3 * half + dy)
                pieces[start : start + out_rows, :] = block[:, 128 * half : 128 * half + 128].astype(BF)
    send_pieces(range(6))

    grad_all[:, :32] = gradient(256, 288)
    for other in range(ydim):
        tails = [grad_all[96 * dy + out_rows * other : 96 * dy + out_rows * (other + 1), :32] for dy in range(3)]
        tails.append(jnp.zeros_like(tails[0]))
        start = block_rows * other + 6 * out_rows
        pieces[start : start + out_rows, :] = jnp.concatenate(tails, axis=1).astype(BF)
    send_pieces(range(6, 8))

    for half in range(2):
        for h in range(2):
            rows = [lat_dense[16 * half + 8 * h + i] for i in range(8)]
            for i, row in enumerate(swap_blocks(rows, lane)):
                lat_tiles[8 * half + i, :, 128 * h : 128 * h + 128] = row.astype(BF)
    for k in range(12):
        held = lat_tiles[tiles_ref[0, k]]
        lat_ref[k] = jnp.where(k < count, held, jnp.zeros_like(held))

    for cond, make in pend:
        @pl.when(cond)
        def _(make=make):
            make().wait_send()

    @pl.loop(0, tdim - 1)
    def _(f):
        @pl.when(t != f + 1)
        def _():
            arrived(ctx_out.at[f], ctx_send.at[f])

        @pl.when((t == 0) | (t == tdim - 1))
        def _():
            arrived(ctx_out.at[f, 0], ctx_edge_send.at[f])

    def add_up(size):
        start = owned_from(t)
        mine = pl.ds(start, size)
        used = pl.ds(0, size)
        parts[spot, used] = pieces[pl.ds(block_rows * y + start, size)]
        arrived(parts.at[pl.ds(0, plane - 1), used], piece_recv)
        total = parts[0, used].astype(F32)
        for i in range(1, plane):
            total = total + parts[i, used].astype(F32)
        z_in[b, used] = total.astype(BF)
        for d in sorted(range(1, zdim), key=lambda d: -min(d, zdim - d)):
            remote(
                z_in.at[b, used], z_in.at[b, used], z_send.at[d], z_recv, tile=lax.rem(b + d, zdim)
            ).start()
        arrived(pieces.at[pl.ds(0, block_rows * ydim - size)], piece_send)
        arrived(z_in.at[pl.ds(0, zdim - 1), used], z_recv)
        total = z_in[0, used].astype(F32)
        for i in range(1, zdim):
            total = total + z_in[i, used].astype(F32)
        final[mine] = total
        for d in range(1, tdim):
            remote(
                final.at[mine], final.at[mine], final_send.at[d - 1], final_recv.at[t], tm=lax.rem(t + d, tdim)
            ).start()
        for d in range(1, zdim):
            arrived(z_in.at[b, used], z_send.at[d])

    for size, has in sized(t, range(8)):
        @pl.when(has)
        def _(size=size):
            add_up(size)

    for l in range(8):
        @pl.when(t != l)
        def _():
            arrived(final.at[pl.ds(sum(shared[:l]), shared[l])], final_recv.at[l])

    for dy in range(3):
        at = [out_rows * dy, out_rows * (3 + dy), out_rows * 6]
        columns = [final[a : a + out_rows, :] for a in at]
        columns[2] = columns[2][:, 32 * dy : 32 * (dy + 1)]
        grad_ref[:, 288 * dy : 288 * (dy + 1)] = jnp.concatenate(columns, axis=1)

    for size, has in sized(t, range(8)):
        @pl.when(has)
        def _(size=size):
            for d in range(1, tdim):
                arrived(final.at[pl.ds(0, size)], final_send.at[d - 1])


def body(sizes, frames_in, w_in, gate_bias, w_ent, active_tiles, active_count, cotangent):
    ydim, tdim, zdim = sizes
    plane = ydim * tdim
    per = 32 // tdim
    out_rows = 96 // ydim
    shared = shares(out_rows)
    vmem = pl.BlockSpec(memory_space=pltpu.VMEM)
    hbm = pl.BlockSpec(memory_space=pltpu.HBM)
    dma = pltpu.SemaphoreType.DMA
    latent, grad = pl.pallas_call(
        functools.partial(kernel, sizes),
        out_shape=(
            jax.ShapeDtypeStruct((12, 48, 256), BF),
            jax.ShapeDtypeStruct((out_rows, 864), F32),
        ),
        in_specs=[hbm] * 7,
        out_specs=(vmem, vmem),
        scratch_shapes=[
            pltpu.VMEM((96, 432), BF),
            pltpu.VMEM((1, 48), F32),
            pltpu.VMEM((96, 864), BF),
            pltpu.SMEM((1, 12), jnp.int32),
            pltpu.SMEM((1, 1, 1), jnp.int32),
            pltpu.VMEM((48, 32, 128), BF),
            pltpu.VMEM((48 * 32, 128), F32),
            pltpu.VMEM((34, 48, 128), BF),
            pltpu.VMEM((12, 48, 256), BF),
            pltpu.VMEM((tdim, per + 2, 48, 128), BF),
            pltpu.VMEM((tdim, 48, 128), BF),
            pltpu.VMEM((2, 48, 128), BF),
            pltpu.VMEM(((per + 2) * 144, 128), BF),
            pltpu.VMEM((tdim - 1, 48, per * 128), F32),
            pltpu.VMEM((tdim - 1, 48, per * 128), F32),
            pltpu.VMEM((48, per * 128), F32),
            pltpu.VMEM((tdim - 1, per, 48, 128), BF),
            pltpu.VMEM((34, 48, 128), BF),
            pltpu.VMEM((2, 48, 128), BF),
            pltpu.VMEM((2, 96, 432), BF),
            pltpu.VMEM((2, 96, 2048), F32),
            pltpu.VMEM((34 * 288, 128), BF),
            pltpu.VMEM((32, 48, 128), F32),
            pltpu.VMEM((36 * 96, 128), BF),
            pltpu.VMEM((32, 48, 128), F32),
            pltpu.VMEM((16, 48, 256), BF),
            pltpu.VMEM((288, 256), F32),
            pltpu.VMEM((ydim * sum(shared), 128), BF),
            pltpu.VMEM((plane, max(shared), 128), BF),
            pltpu.VMEM((zdim, max(shared), 128), BF),
            pltpu.VMEM((sum(shared), 128), F32),
            dma((7,)),
            dma((tdim,)), dma((tdim,)),
            dma((2,)), dma((tdim,)),
            dma((2,)), dma((2,)),
            dma((tdim - 1,)), dma((tdim,)),
            dma((tdim - 1,)), dma((2,)),
            dma, dma,
            dma((zdim,)), dma,
            dma((tdim - 1,)), dma((tdim,)),
            pltpu.SemaphoreType.REGULAR((len(relay_strides(zdim)) + 1,)),
        ],
        compiler_params=pltpu.CompilerParams(
            collective_id=0, has_side_effects=True, vmem_limit_bytes=32 * 1024 * 1024
        ),
        cost_estimate=pl.CostEstimate(flops=1_700_000_000, bytes_accessed=1_500_000, transcendentals=1_500_000),
        name="coding_window",
    )(
        pltpu.with_memory_space_constraint(frames_in[0, 0], pltpu.HBM),
        pltpu.with_memory_space_constraint(w_in, pltpu.HBM),
        pltpu.with_memory_space_constraint(gate_bias[None], pltpu.HBM),
        pltpu.with_memory_space_constraint(w_ent, pltpu.HBM),
        pltpu.with_memory_space_constraint(active_tiles[0, 0], pltpu.HBM),
        active_count,
        pltpu.with_memory_space_constraint(cotangent[0, 0, 0], pltpu.HBM),
    )
    return (latent[None, None, None], grad)


def solution(mesh):
    sizes = tuple(mesh.shape[axis] for axis in ("dp", "tm", "tile"))
    return jax.shard_map(
        functools.partial(body, sizes),
        mesh=mesh,
        in_specs=(
            P("dp", "tm", None, "tile", None),
            P(),
            P(),
            P(),
            P("dp", "tm", "tile", None),
            P("dp", "tm", "tile"),
            P("dp", "tm", "tile", None, None, None),
        ),
        out_specs=(P("dp", "tm", "tile", None, None, None), P("dp", None)),
        check_vma=False,
    )
```

```python
import functools

import jax
import jax.numpy as jnp
from jax import lax
from jax.experimental import pallas as pl
from jax.experimental.pallas import tpu as pltpu
from jax.sharding import PartitionSpec as P

BF = jnp.bfloat16
F32 = jnp.float32
MESH = pl.DeviceIdType.MESH


NEAR = 2


def relay_strides(size):
    strides, known = [], NEAR
    while known < size // 2:
        strides.append(known)
        known *= 2
    return strides


def shares(out_rows):
    first, last = 6 * out_rows // 16, -(-out_rows // 16)
    return [16 * (first * (i + 1) // 6 - first * i // 6) for i in range(6)] + [
        16 * (last * (i + 1) // 2 - last * i // 2) for i in range(2)
    ]


def swap_blocks(parts, lane):
    for m in (1, 2, 4):
        low = (lane & (16 * m)) == 0
        done = list(parts)
        for p in range(8):
            if p & m:
                continue
            q = p | m
            done[p] = jnp.where(low, parts[p], pltpu.roll(parts[q], 16 * m, 1))
            done[q] = jnp.where(low, pltpu.roll(parts[p], 128 - 16 * m, 1), parts[q])
        parts = done
    return parts


def store_shifts(out_ref, start, gap, value, lane):
    wide = value.astype(F32)
    before = jnp.where(lane == 0, 0.0, pltpu.roll(wide, 1, 1))
    after = jnp.where(lane == 127, 0.0, pltpu.roll(wide, 127, 1))
    out_ref[pl.ds(start, 48), :] = before.astype(BF)
    out_ref[pl.ds(start + gap, 48), :] = value
    out_ref[pl.ds(start + 2 * gap, 48), :] = after.astype(BF)


def kernel(
    sizes,
    x_hbm, w_in_hbm, bias_hbm, w_ent_hbm, tiles_hbm, count_hbm, cot_hbm,
    lat_ref, grad_ref,
    w_in_ref, bias_ref, w_ent_ref, tiles_ref, count_ref,
    xv, xf, xb, cotv, frame_rows, edge_rows, halo, conv_in, gates, drives, state, ctx_out, ctx, ctx_edge,
    w_part, pre_x, joined, cot_dense, push, lat_dense, lat_tiles, grad_all, pieces, parts, z_in, final,
    load_sem, main_send, main_recv, edge_send, edge_recv, halo_send, halo_recv,
    ctx_send, ctx_recv, ctx_edge_send, ctx_edge_recv,
    piece_send, piece_recv, z_send, z_recv, final_send, final_recv, relay_sem,
):
    ydim, tdim, zdim = sizes
    y = lax.axis_index("dp")
    t = lax.axis_index("tm")
    b = lax.axis_index("tile")
    above = lax.rem(b + zdim - 1, zdim)
    below = lax.rem(b + 1, zdim)
    plane = ydim * tdim
    spot = y * tdim + t
    per = 32 // tdim
    strides = relay_strides(zdim)
    out_rows = 96 // ydim
    shared = shares(out_rows)
    block_rows = sum(shared)
    pend = []

    def send(cond, make):
        @pl.when(cond)
        def _():
            make().start()

        pend.append((cond, make))

    def remote(src, dst, ssem, rsem, **where):
        return pltpu.make_async_remote_copy(
            src_ref=src, dst_ref=dst, send_sem=ssem, recv_sem=rsem, device_id=where, device_id_type=MESH
        )

    def arrived(ref, sem):
        pltpu.make_async_copy(ref, ref, sem).wait()

    loads = [
        pltpu.make_async_copy(src, dst, load_sem.at[i])
        for i, (src, dst) in enumerate(
            (
                (x_hbm, xv), (tiles_hbm, tiles_ref), (count_hbm, count_ref), (cot_hbm, cotv),
                (w_in_hbm, w_in_ref), (bias_hbm, bias_ref), (w_ent_hbm, w_ent_ref),
            )
        )
    ]
    loads[0].start()

    barrier = pltpu.get_barrier_semaphore()

    greeted = 0
    for axis, size, offsets in (
        ("tm", tdim, range(1, tdim)),
        ("tile", zdim, [d for d in range(1, zdim) if min(d, zdim - d) <= NEAR]),
        ("dp", ydim, range(1, ydim)),
    ):
        for d in offsets:
            peer = lax.rem(lax.axis_index(axis) + d, size)
            pl.semaphore_signal(barrier, inc=1, device_id={axis: peer}, device_id_type=MESH)
            greeted += 1

    for load in loads[1:]:
        load.start()
    lane = lax.broadcasted_iota(jnp.int32, (48, 128), 1)
    blank = jnp.zeros((48, 128), BF)

    loads[0].wait()
    xf[...] = xv[...].astype(F32).reshape(48 * 32, 128)
    xb[0] = blank
    xb[33] = blank
    for r in range(32):
        xb[1 + r] = xf[pl.ds(r, 48, stride=32), :].astype(BF)

    pl.semaphore_wait(barrier, greeted)

    def relay(step, axis, size, offsets):
        for d in offsets:
            peer = lax.rem(lax.axis_index(axis) + d, size)
            pl.semaphore_signal(relay_sem.at[step], inc=1, device_id={axis: peer}, device_id_type=MESH)

    sends = t < tdim - 1
    always = t >= 0
    send(always, lambda: remote(xb.at[32], halo.at[0], halo_send.at[0], halo_recv.at[0], tile=below))
    send(always, lambda: remote(xb.at[1], halo.at[1], halo_send.at[1], halo_recv.at[1], tile=above))
    for d in range(1, tdim):
        j = lax.rem(t + tdim - d, tdim)
        send(
            sends,
            lambda d=d, j=j: remote(
                xb.at[pl.ds(per * j, per + 2)], frame_rows.at[t], main_send.at[d], main_recv.at[t], tm=j
            ),
        )
    relay(len(strides), "dp", ydim, range(1, ydim))
    if strides:
        relay(0, "tile", zdim, (strides[0], zdim - strides[0]))

    @pl.when(sends)
    def _():
        frame_rows[t] = xb[pl.ds(per * t, per + 2)]

    for r in range(1, 33):
        store_shifts(joined, 288 * r, 96, xb[r], lane)

    for load in loads[1:4]:
        load.wait()
    count = count_ref[0, 0, 0]
    slots = []
    for n in range(16):
        found = jnp.int32(0)
        for k in range(12):
            found = jnp.where((tiles_ref[0, k] == n) & (k < count), k + 1, found)
        slots.append(found)
    for half in range(2):
        for h in range(2):
            columns = slice(128 * h, 128 * h + 128)
            rows = []
            for i in range(8):
                found = slots[8 * half + i]
                held = cotv[jnp.maximum(found - 1, 0), :, columns].astype(F32)
                rows.append(jnp.where(found > 0, held, 0.0))
            for i, row in enumerate(swap_blocks(rows, lane)):
                cot_dense[16 * half + 8 * h + i] = row

    for edge, row, there in ((0, 0, b > 0), (1, 33, b < zdim - 1)):
        arrived(halo.at[edge], halo_recv.at[edge])
        end = edge * (tdim - 1)
        send(
            sends & (t != end),
            lambda edge=edge, end=end: remote(
                halo.at[edge], edge_rows.at[t], edge_send.at[edge], edge_recv.at[t], tm=end
            ),
        )
        store_shifts(joined, 288 * row, 96, jnp.where(there, halo[edge], blank), lane)

    @pl.when(t == 0)
    def _():
        edge_rows[0] = halo[0]

    loads[6].wait()
    w_all = w_ent_ref[...]
    for part in range(2):
        w_part[part] = jnp.concatenate([w_all[:, 96 * k + 48 * part : 96 * k + 48 * part + 48] for k in range(9)], axis=1)

    def taps(part, r):
        starts = [288 * (r + dy) + 96 * dx + 48 * part for dy in range(3) for dx in range(3)]
        return jnp.concatenate([joined[start : start + 48, :] for start in starts], axis=0)

    for block in range(2):
        cells = jnp.concatenate([taps(0, 16 * block + r) for r in range(16)], axis=1)
        pre_x[block] = jnp.dot(w_part[0], cells, preferred_element_type=F32)

    for step in range(1, len(strides)):
        pl.semaphore_wait(relay_sem.at[step - 1], 2)
        relay(step, "tile", zdim, (strides[step], zdim - strides[step]))

    state[...] = jnp.zeros_like(state)
    for load in loads[4:6]:
        load.wait()
    bias = bias_ref[...].T[:48, :1]

    def convolve(f):
        @pl.when(t != f)
        def _():
            arrived(frame_rows.at[f], main_recv.at[f])

        for end, row, there in ((0, 0, b > 0), (tdim - 1, per + 1, b < zdim - 1)):
            @pl.when(t == end)
            def _():
                @pl.when(f != end)
                def _():
                    arrived(edge_rows.at[f], edge_recv.at[f])

                frame_rows[f, row] = jnp.where(there, edge_rows[f], blank)

        for r in range(per + 2):
            store_shifts(conv_in, 144 * r, 48, frame_rows[f, r], lane)
        cells = jnp.concatenate([conv_in[pl.ds(144 * r, 432), :] for r in range(per)], axis=1)
        mixed = jnp.dot(w_in_ref[...], cells, preferred_element_type=F32)
        gates[f] = 0.5 * jnp.tanh(0.5 * (mixed[:48] + bias)) + 0.5
        drives[f] = jnp.tanh(mixed[48:])

    def advance(f):
        now = gates[f] * state[...] + drives[f]
        state[...] = now
        for r in range(per):
            ctx_out[f, r] = now[:, 128 * r : 128 * r + 128].astype(BF)

        @pl.when(t != f + 1)
        def _():
            remote(
                ctx_out.at[f], ctx.at[pl.ds(1 + per * t, per)], ctx_send.at[f], ctx_recv.at[t], tm=f + 1
            ).start()

        @pl.when(t == f + 1)
        def _():
            ctx[pl.ds(1 + per * t, per)] = ctx_out[f]

        @pl.when(t == tdim - 1)
        def _():
            remote(
                ctx_out.at[f, per - 1], ctx_edge.at[0], ctx_edge_send.at[f], ctx_edge_recv.at[0],
                tm=f + 1, tile=below,
            ).start()

        @pl.when(t == 0)
        def _():
            remote(
                ctx_out.at[f, 0], ctx_edge.at[1], ctx_edge_send.at[f], ctx_edge_recv.at[1],
                tm=f + 1, tile=above,
            ).start()

    @pl.loop(0, tdim)
    def _(i):
        f = lax.rem(t + i, tdim)

        @pl.when(f < tdim - 1)
        def _():
            convolve(f)

            @pl.when((f < t) | (t == 0))
            def _():
                advance(f)

    @pl.loop(0, tdim - 1)
    def _(f):
        @pl.when((f >= t) & (t > 0))
        def _():
            advance(f)

    if strides:
        pl.semaphore_wait(relay_sem.at[len(strides) - 1], 2)
    if ydim > 1:
        pl.semaphore_wait(relay_sem.at[len(strides)], ydim - 1)

    @pl.when(t == 0)
    def _():
        ctx[...] = jnp.zeros_like(ctx)
        ctx_edge[...] = jnp.zeros_like(ctx_edge)

    for j in range(tdim):
        @pl.when((t > 0) & (t != j))
        def _():
            arrived(ctx.at[pl.ds(1 + per * j, per)], ctx_recv.at[j])

        for r in range(1 + per * j, 1 + per * (j + 1)):
            store_shifts(joined, 288 * r + 48, 96, ctx[r], lane)

    for edge, row, there in ((0, 0, b > 0), (1, 33, b < zdim - 1)):
        @pl.when(t > 0)
        def _():
            arrived(ctx_edge.at[edge], ctx_edge_recv.at[edge])

        store_shifts(joined, 288 * row + 48, 96, jnp.where(there, ctx_edge[edge], blank), lane)

    for r in (-2, -1, 32, 33):
        push[96 * (33 - r) : 96 * (34 - r), :] = jnp.zeros((96, 128), BF)
    for block in range(2):
        cells = jnp.concatenate([taps(1, 16 * block + r) for r in range(16)], axis=1)
        pre = pre_x[block] + jnp.dot(w_part[1], cells, preferred_element_type=F32)
        for i in range(16):
            r = 16 * block + i
            mean = pre[:48, 128 * i : 128 * i + 128]
            spread = pre[48:, 128 * i : 128 * i + 128]
            small = jnp.exp(-jnp.abs(spread))
            sigma = 0.5 + jnp.maximum(spread, 0.0) + jnp.log(1.0 + small)
            slope = jnp.where(spread >= 0, 1.0, small) / (1.0 + small)
            scale = 1.0 / sigma
            lat = (xb[r + 1].astype(F32) - mean) * scale
            lat_dense[r] = lat
            near = -cot_dense[r] * scale
            push[96 * (33 - r) : 96 * (33 - r) + 48, :] = near.astype(BF)
            push[96 * (33 - r) + 48 : 96 * (34 - r), :] = (near * lat * slope).astype(BF)

    near = jnp.concatenate([push[96 * (33 - r) : 96 * (36 - r), :] for r in range(34)], axis=1)

    def gradient(first, last):
        rows = jnp.concatenate([joined[288 * r + first : 288 * r + last, :] for r in range(34)], axis=1)
        return lax.dot_general(near, rows, (((1,), (1,)), ((), ())), preferred_element_type=F32)

    def owned_from(l):
        return pl.multiple_of(sum(shared[k] * ((l + 7 - k) // 8) for k in range(7)), 16)

    def sized(l, among):
        for size in sorted({shared[k] for k in among}):
            has = l < 0
            for k in among:
                if shared[k] == size:
                    has = has | (l == k)
            yield size, has

    def send_piece(other, l, size):
        src = pieces.at[pl.ds(block_rows * other + owned_from(l), size)]
        remote(src, parts.at[spot, pl.ds(0, size)], piece_send, piece_recv, dp=other, tm=l).start()

    def send_pieces(among):
        for dy in sorted(range(ydim), key=lambda dy: -min(dy, ydim - dy)):
            @pl.loop(0, tdim)
            def _(i):
                l = lax.rem(t + tdim // 2 + i, tdim)
                for size, has in sized(l, among):
                    @pl.when(has & (l != t) if dy == 0 else has)
                    def _():
                        send_piece(lax.rem(y + dy, ydim), l, size)

    grad_all[...] = gradient(0, 256)
    for other in range(ydim):
        for dy in range(3):
            block = grad_all[96 * dy + out_rows * other : 96 * dy + out_rows * (other + 1), :]
            for half in range(2):
                start = block_rows * other + out_rows * (3 * half + dy)
                pieces[start : start + out_rows, :] = block[:, 128 * half : 128 * half + 128].astype(BF)
    send_pieces(range(6))

    grad_all[:, :32] = gradient(256, 288)
    for other in range(ydim):
        tails = [grad_all[96 * dy + out_rows * other : 96 * dy + out_rows * (other + 1), :32] for dy in range(3)]
        tails.append(jnp.zeros_like(tails[0]))
        start = block_rows * other + 6 * out_rows
        pieces[start : start + out_rows, :] = jnp.concatenate(tails, axis=1).astype(BF)
    send_pieces(range(6, 8))

    for half in range(2):
        for h in range(2):
            rows = [lat_dense[16 * half + 8 * h + i] for i in range(8)]
            for i, row in enumerate(swap_blocks(rows, lane)):
                lat_tiles[8 * half + i, :, 128 * h : 128 * h + 128] = row.astype(BF)
    for k in range(12):
        held = lat_tiles[tiles_ref[0, k]]
        lat_ref[k] = jnp.where(k < count, held, jnp.zeros_like(held))

    for cond, make in pend:
        @pl.when(cond)
        def _(make=make):
            make().wait_send()

    @pl.loop(0, tdim - 1)
    def _(f):
        @pl.when(t != f + 1)
        def _():
            arrived(ctx_out.at[f], ctx_send.at[f])

        @pl.when((t == 0) | (t == tdim - 1))
        def _():
            arrived(ctx_out.at[f, 0], ctx_edge_send.at[f])

    def add_up(size):
        start = owned_from(t)
        mine = pl.ds(start, size)
        used = pl.ds(0, size)
        parts[spot, used] = pieces[pl.ds(block_rows * y + start, size)]
        arrived(parts.at[pl.ds(0, plane - 1), used], piece_recv)
        total = parts[0, used].astype(F32)
        for i in range(1, plane):
            total = total + parts[i, used].astype(F32)
        z_in[b, used] = total.astype(BF)

        @pl.loop(0, zdim - 1)
        def _(i):
            d = zdim // 2 + i // 2 - lax.rem(i, 2) * (2 * (i // 2) + 1)
            remote(
                z_in.at[b, used], z_in.at[b, used], z_send.at[d], z_recv, tile=lax.rem(b + d, zdim)
            ).start()

        arrived(pieces.at[pl.ds(0, block_rows * ydim - size)], piece_send)
        arrived(z_in.at[pl.ds(0, zdim - 1), used], z_recv)
        total = z_in[0, used].astype(F32)
        for i in range(1, zdim):
            total = total + z_in[i, used].astype(F32)
        final[mine] = total
        for d in range(1, tdim):
            remote(
                final.at[mine], final.at[mine], final_send.at[d - 1], final_recv.at[t], tm=lax.rem(t + d, tdim)
            ).start()

        @pl.loop(1, zdim)
        def _(d):
            arrived(z_in.at[b, used], z_send.at[d])

    for size, has in sized(t, range(8)):
        @pl.when(has)
        def _(size=size):
            add_up(size)

    for l in range(8):
        @pl.when(t != l)
        def _():
            arrived(final.at[pl.ds(sum(shared[:l]), shared[l])], final_recv.at[l])

    for dy in range(3):
        at = [out_rows * dy, out_rows * (3 + dy), out_rows * 6]
        columns = [final[a : a + out_rows, :] for a in at]
        columns[2] = columns[2][:, 32 * dy : 32 * (dy + 1)]
        grad_ref[:, 288 * dy : 288 * (dy + 1)] = jnp.concatenate(columns, axis=1)

    for size, has in sized(t, range(8)):
        @pl.when(has)
        def _(size=size):
            for d in range(1, tdim):
                arrived(final.at[pl.ds(0, size)], final_send.at[d - 1])


def body(sizes, frames_in, w_in, gate_bias, w_ent, active_tiles, active_count, cotangent):
    ydim, tdim, zdim = sizes
    plane = ydim * tdim
    per = 32 // tdim
    out_rows = 96 // ydim
    shared = shares(out_rows)
    vmem = pl.BlockSpec(memory_space=pltpu.VMEM)
    hbm = pl.BlockSpec(memory_space=pltpu.HBM)
    dma = pltpu.SemaphoreType.DMA
    latent, grad = pl.pallas_call(
        functools.partial(kernel, sizes),
        out_shape=(
            jax.ShapeDtypeStruct((12, 48, 256), BF),
            jax.ShapeDtypeStruct((out_rows, 864), F32),
        ),
        in_specs=[hbm] * 7,
        out_specs=(vmem, vmem),
        scratch_shapes=[
            pltpu.VMEM((96, 432), BF),
            pltpu.VMEM((1, 48), F32),
            pltpu.VMEM((96, 864), BF),
            pltpu.SMEM((1, 12), jnp.int32),
            pltpu.SMEM((1, 1, 1), jnp.int32),
            pltpu.VMEM((48, 32, 128), BF),
            pltpu.VMEM((48 * 32, 128), F32),
            pltpu.VMEM((34, 48, 128), BF),
            pltpu.VMEM((12, 48, 256), BF),
            pltpu.VMEM((tdim, per + 2, 48, 128), BF),
            pltpu.VMEM((tdim, 48, 128), BF),
            pltpu.VMEM((2, 48, 128), BF),
            pltpu.VMEM(((per + 2) * 144, 128), BF),
            pltpu.VMEM((tdim - 1, 48, per * 128), F32),
            pltpu.VMEM((tdim - 1, 48, per * 128), F32),
            pltpu.VMEM((48, per * 128), F32),
            pltpu.VMEM((tdim - 1, per, 48, 128), BF),
            pltpu.VMEM((34, 48, 128), BF),
            pltpu.VMEM((2, 48, 128), BF),
            pltpu.VMEM((2, 96, 432), BF),
            pltpu.VMEM((2, 96, 2048), F32),
            pltpu.VMEM((34 * 288, 128), BF),
            pltpu.VMEM((32, 48, 128), F32),
            pltpu.VMEM((36 * 96, 128), BF),
            pltpu.VMEM((32, 48, 128), F32),
            pltpu.VMEM((16, 48, 256), BF),
            pltpu.VMEM((288, 256), F32),
            pltpu.VMEM((ydim * sum(shared), 128), BF),
            pltpu.VMEM((plane, max(shared), 128), BF),
            pltpu.VMEM((zdim, max(shared), 128), BF),
            pltpu.VMEM((sum(shared), 128), F32),
            dma((7,)),
            dma((tdim,)), dma((tdim,)),
            dma((2,)), dma((tdim,)),
            dma((2,)), dma((2,)),
            dma((tdim - 1,)), dma((tdim,)),
            dma((tdim - 1,)), dma((2,)),
            dma, dma,
            dma((zdim,)), dma,
            dma((tdim - 1,)), dma((tdim,)),
            pltpu.SemaphoreType.REGULAR((len(relay_strides(zdim)) + 1,)),
        ],
        compiler_params=pltpu.CompilerParams(
            collective_id=0, has_side_effects=True, vmem_limit_bytes=32 * 1024 * 1024
        ),
        cost_estimate=pl.CostEstimate(flops=1_700_000_000, bytes_accessed=1_500_000, transcendentals=1_500_000),
        name="coding_window",
    )(
        pltpu.with_memory_space_constraint(frames_in[0, 0], pltpu.HBM),
        pltpu.with_memory_space_constraint(w_in, pltpu.HBM),
        pltpu.with_memory_space_constraint(gate_bias[None], pltpu.HBM),
        pltpu.with_memory_space_constraint(w_ent, pltpu.HBM),
        pltpu.with_memory_space_constraint(active_tiles[0, 0], pltpu.HBM),
        active_count,
        pltpu.with_memory_space_constraint(cotangent[0, 0, 0], pltpu.HBM),
    )
    return (latent[None, None, None], grad)


def solution(mesh):
    sizes = tuple(mesh.shape[axis] for axis in ("dp", "tm", "tile"))
    return jax.shard_map(
        functools.partial(body, sizes),
        mesh=mesh,
        in_specs=(
            P("dp", "tm", None, "tile", None),
            P(),
            P(),
            P(),
            P("dp", "tm", "tile", None),
            P("dp", "tm", "tile"),
            P("dp", "tm", "tile", None, None, None),
        ),
        out_specs=(P("dp", "tm", "tile", None, None, None), P("dp", None)),
        check_vma=False,
    )
```

```python
import functools

import jax
import jax.numpy as jnp
from jax import lax
from jax.experimental import pallas as pl
from jax.experimental.pallas import tpu as pltpu
from jax.sharding import PartitionSpec as P

BF = jnp.bfloat16
F32 = jnp.float32
MESH = pl.DeviceIdType.MESH


NEAR = 2


def relay_strides(size):
    strides, known = [], NEAR
    while known < size // 2:
        strides.append(known)
        known *= 2
    return strides


def shares(out_rows):
    first, last = 6 * out_rows // 16, -(-out_rows // 16)
    return [16 * (first * (i + 1) // 6 - first * i // 6) for i in range(6)] + [
        16 * (last * (i + 1) // 2 - last * i // 2) for i in range(2)
    ]


def swap_blocks(parts, lane):
    for m in (1, 2, 4):
        low = (lane & (16 * m)) == 0
        done = list(parts)
        for p in range(8):
            if p & m:
                continue
            q = p | m
            done[p] = jnp.where(low, parts[p], pltpu.roll(parts[q], 16 * m, 1))
            done[q] = jnp.where(low, pltpu.roll(parts[p], 128 - 16 * m, 1), parts[q])
        parts = done
    return parts


def store_shifts(out_ref, start, gap, value, lane):
    wide = value.astype(F32)
    before = jnp.where(lane == 0, 0.0, pltpu.roll(wide, 1, 1))
    after = jnp.where(lane == 127, 0.0, pltpu.roll(wide, 127, 1))
    out_ref[pl.ds(start, 48), :] = before.astype(BF)
    out_ref[pl.ds(start + gap, 48), :] = value
    out_ref[pl.ds(start + 2 * gap, 48), :] = after.astype(BF)


def kernel(
    sizes,
    x_hbm, w_in_hbm, bias_hbm, w_ent_hbm, tiles_hbm, count_hbm, cot_hbm,
    lat_ref, grad_ref,
    w_in_ref, bias_ref, w_ent_ref, tiles_ref, count_ref,
    xv, xf, xb, cotv, frame_rows, edge_rows, halo, conv_in, gates, drives, state, ctx_out, ctx, ctx_edge,
    w_part, pre_x, joined, cot_dense, push, lat_dense, lat_tiles, grad_all, pieces, parts, z_in, final,
    load_sem, main_send, main_recv, edge_send, edge_recv, halo_send, halo_recv,
    ctx_send, ctx_recv, ctx_edge_send, ctx_edge_recv,
    piece_send, piece_recv, z_send, z_recv, final_send, final_recv, relay_sem,
):
    ydim, tdim, zdim = sizes
    y = lax.axis_index("dp")
    t = lax.axis_index("tm")
    b = lax.axis_index("tile")
    above = lax.rem(b + zdim - 1, zdim)
    below = lax.rem(b + 1, zdim)
    plane = ydim * tdim
    spot = y * tdim + t
    per = 32 // tdim
    strides = relay_strides(zdim)
    out_rows = 96 // ydim
    shared = shares(out_rows)
    block_rows = sum(shared)
    pend = []

    def send(cond, make):
        @pl.when(cond)
        def _():
            make().start()

        pend.append((cond, make))

    def remote(src, dst, ssem, rsem, **where):
        return pltpu.make_async_remote_copy(
            src_ref=src, dst_ref=dst, send_sem=ssem, recv_sem=rsem, device_id=where, device_id_type=MESH
        )

    def arrived(ref, sem):
        pltpu.make_async_copy(ref, ref, sem).wait()

    loads = [
        pltpu.make_async_copy(src, dst, load_sem.at[i])
        for i, (src, dst) in enumerate(
            (
                (x_hbm, xv), (tiles_hbm, tiles_ref), (count_hbm, count_ref), (cot_hbm, cotv),
                (w_in_hbm, w_in_ref), (bias_hbm, bias_ref), (w_ent_hbm, w_ent_ref),
            )
        )
    ]
    loads[0].start()

    barrier = pltpu.get_barrier_semaphore()

    greeted = 0
    for axis, size, offsets in (
        ("tm", tdim, range(1, tdim)),
        ("tile", zdim, [d for d in range(1, zdim) if min(d, zdim - d) <= NEAR]),
        ("dp", ydim, range(1, ydim)),
    ):
        for d in offsets:
            peer = lax.rem(lax.axis_index(axis) + d, size)
            pl.semaphore_signal(barrier, inc=1, device_id={axis: peer}, device_id_type=MESH)
            greeted += 1

    for load in loads[1:]:
        load.start()
    lane = lax.broadcasted_iota(jnp.int32, (48, 128), 1)
    blank = jnp.zeros((48, 128), BF)

    loads[0].wait()
    xf[...] = xv[...].astype(F32).reshape(48 * 32, 128)
    xb[0] = blank
    xb[33] = blank
    for r in range(32):
        xb[1 + r] = xf[pl.ds(r, 48, stride=32), :].astype(BF)

    pl.semaphore_wait(barrier, greeted)

    def relay(step, axis, size, offsets):
        for d in offsets:
            peer = lax.rem(lax.axis_index(axis) + d, size)
            pl.semaphore_signal(relay_sem.at[step], inc=1, device_id={axis: peer}, device_id_type=MESH)

    sends = t < tdim - 1
    always = t >= 0
    send(always, lambda: remote(xb.at[32], halo.at[0], halo_send.at[0], halo_recv.at[0], tile=below))
    send(always, lambda: remote(xb.at[1], halo.at[1], halo_send.at[1], halo_recv.at[1], tile=above))
    for d in range(1, tdim):
        j = lax.rem(t + tdim - d, tdim)
        send(
            sends,
            lambda d=d, j=j: remote(
                xb.at[pl.ds(per * j, per + 2)], frame_rows.at[t], main_send.at[d], main_recv.at[t], tm=j
            ),
        )
    relay(len(strides), "dp", ydim, range(1, ydim))
    if strides:
        relay(0, "tile", zdim, (strides[0], zdim - strides[0]))

    @pl.when(sends)
    def _():
        frame_rows[t] = xb[pl.ds(per * t, per + 2)]

    for r in range(1, 33):
        store_shifts(joined, 288 * r, 96, xb[r], lane)

    for load in loads[1:4]:
        load.wait()
    count = count_ref[0, 0, 0]
    slots = []
    for n in range(16):
        found = jnp.int32(0)
        for k in range(12):
            found = jnp.where((tiles_ref[0, k] == n) & (k < count), k + 1, found)
        slots.append(found)
    for half in range(2):
        for h in range(2):
            columns = slice(128 * h, 128 * h + 128)
            rows = []
            for i in range(8):
                found = slots[8 * half + i]
                held = cotv[jnp.maximum(found - 1, 0), :, columns].astype(F32)
                rows.append(jnp.where(found > 0, held, 0.0))
            for i, row in enumerate(swap_blocks(rows, lane)):
                cot_dense[16 * half + 8 * h + i] = row

    for edge, row, there in ((0, 0, b > 0), (1, 33, b < zdim - 1)):
        arrived(halo.at[edge], halo_recv.at[edge])
        end = edge * (tdim - 1)
        send(
            sends & (t != end),
            lambda edge=edge, end=end: remote(
                halo.at[edge], edge_rows.at[t], edge_send.at[edge], edge_recv.at[t], tm=end
            ),
        )
        store_shifts(joined, 288 * row, 96, jnp.where(there, halo[edge], blank), lane)

    @pl.when(t == 0)
    def _():
        edge_rows[0] = halo[0]

    loads[6].wait()
    w_all = w_ent_ref[...]
    for part in range(2):
        w_part[part] = jnp.concatenate([w_all[:, 96 * k + 48 * part : 96 * k + 48 * part + 48] for k in range(9)], axis=1)

    def taps(part, r):
        starts = [288 * (r + dy) + 96 * dx + 48 * part for dy in range(3) for dx in range(3)]
        return jnp.concatenate([joined[start : start + 48, :] for start in starts], axis=0)

    for block in range(2):
        cells = jnp.concatenate([taps(0, 16 * block + r) for r in range(16)], axis=1)
        pre_x[block] = jnp.dot(w_part[0], cells, preferred_element_type=F32)

    for step in range(1, len(strides)):
        pl.semaphore_wait(relay_sem.at[step - 1], 2)
        relay(step, "tile", zdim, (strides[step], zdim - strides[step]))

    state[...] = jnp.zeros_like(state)
    for load in loads[4:6]:
        load.wait()
    bias = bias_ref[...].T[:48, :1]

    def convolve(f):
        @pl.when(t != f)
        def _():
            arrived(frame_rows.at[f], main_recv.at[f])

        for end, row, there in ((0, 0, b > 0), (tdim - 1, per + 1, b < zdim - 1)):
            @pl.when(t == end)
            def _():
                @pl.when(f != end)
                def _():
                    arrived(edge_rows.at[f], edge_recv.at[f])

                frame_rows[f, row] = jnp.where(there, edge_rows[f], blank)

        for r in range(per + 2):
            store_shifts(conv_in, 144 * r, 48, frame_rows[f, r], lane)
        cells = jnp.concatenate([conv_in[pl.ds(144 * r, 432), :] for r in range(per)], axis=1)
        mixed = jnp.dot(w_in_ref[...], cells, preferred_element_type=F32)
        gates[f] = 0.5 * jnp.tanh(0.5 * (mixed[:48] + bias)) + 0.5
        drives[f] = jnp.tanh(mixed[48:])

    def advance(f):
        now = gates[f] * state[...] + drives[f]
        state[...] = now
        for r in range(per):
            ctx_out[f, r] = now[:, 128 * r : 128 * r + 128].astype(BF)

        @pl.when(t != f + 1)
        def _():
            remote(
                ctx_out.at[f], ctx.at[pl.ds(1 + per * t, per)], ctx_send.at[f], ctx_recv.at[t], tm=f + 1
            ).start()

        @pl.when(t == f + 1)
        def _():
            ctx[pl.ds(1 + per * t, per)] = ctx_out[f]

        @pl.when(t == tdim - 1)
        def _():
            remote(
                ctx_out.at[f, per - 1], ctx_edge.at[0], ctx_edge_send.at[f], ctx_edge_recv.at[0],
                tm=f + 1, tile=below,
            ).start()

        @pl.when(t == 0)
        def _():
            remote(
                ctx_out.at[f, 0], ctx_edge.at[1], ctx_edge_send.at[f], ctx_edge_recv.at[1],
                tm=f + 1, tile=above,
            ).start()

    @pl.loop(0, tdim)
    def _(i):
        f = lax.rem(t + i, tdim)

        @pl.when(f < tdim - 1)
        def _():
            convolve(f)

            @pl.when((f < t) | (t == 0))
            def _():
                advance(f)

    @pl.loop(0, tdim - 1)
    def _(f):
        @pl.when((f >= t) & (t > 0))
        def _():
            advance(f)

    if strides:
        pl.semaphore_wait(relay_sem.at[len(strides) - 1], 2)
    if ydim > 1:
        pl.semaphore_wait(relay_sem.at[len(strides)], ydim - 1)

    @pl.when(t == 0)
    def _():
        ctx[...] = jnp.zeros_like(ctx)
        ctx_edge[...] = jnp.zeros_like(ctx_edge)

    for j in range(tdim):
        @pl.when((t > 0) & (t != j))
        def _():
            arrived(ctx.at[pl.ds(1 + per * j, per)], ctx_recv.at[j])

        for r in range(1 + per * j, 1 + per * (j + 1)):
            store_shifts(joined, 288 * r + 48, 96, ctx[r], lane)

    for edge, row, there in ((0, 0, b > 0), (1, 33, b < zdim - 1)):
        @pl.when(t > 0)
        def _():
            arrived(ctx_edge.at[edge], ctx_edge_recv.at[edge])

        store_shifts(joined, 288 * row + 48, 96, jnp.where(there, ctx_edge[edge], blank), lane)

    for r in (-2, -1, 32, 33):
        push[96 * (33 - r) : 96 * (34 - r), :] = jnp.zeros((96, 128), BF)
    for block in range(2):
        cells = jnp.concatenate([taps(1, 16 * block + r) for r in range(16)], axis=1)
        pre = pre_x[block] + jnp.dot(w_part[1], cells, preferred_element_type=F32)
        for i in range(16):
            r = 16 * block + i
            mean = pre[:48, 128 * i : 128 * i + 128]
            spread = pre[48:, 128 * i : 128 * i + 128]
            small = jnp.exp(-jnp.abs(spread))
            sigma = 0.5 + jnp.maximum(spread, 0.0) + jnp.log(1.0 + small)
            slope = jnp.where(spread >= 0, 1.0, small) / (1.0 + small)
            scale = 1.0 / sigma
            lat = (xb[r + 1].astype(F32) - mean) * scale
            lat_dense[r] = lat
            near = -cot_dense[r] * scale
            push[96 * (33 - r) : 96 * (33 - r) + 48, :] = near.astype(BF)
            push[96 * (33 - r) + 48 : 96 * (34 - r), :] = (near * lat * slope).astype(BF)

    near = jnp.concatenate([push[96 * (33 - r) : 96 * (36 - r), :] for r in range(34)], axis=1)

    def gradient(first, last):
        rows = jnp.concatenate([joined[288 * r + first : 288 * r + last, :] for r in range(34)], axis=1)
        return lax.dot_general(near, rows, (((1,), (1,)), ((), ())), preferred_element_type=F32)

    def owned_from(l):
        return pl.multiple_of(sum(shared[k] * ((l + 7 - k) // 8) for k in range(7)), 16)

    def sized(l, among):
        for size in sorted({shared[k] for k in among}):
            has = l < 0
            for k in among:
                if shared[k] == size:
                    has = has | (l == k)
            yield size, has

    def send_piece(other, l, size):
        src = pieces.at[pl.ds(block_rows * other + owned_from(l), size)]
        remote(src, parts.at[spot, pl.ds(0, size)], piece_send, piece_recv, dp=other, tm=l).start()

    def hops(way):
        dy, dt = way
        return min(dy, ydim - dy) + min(dt // 2, (tdim - dt) // 2)

    ways = [(dy, dt) for dy in range(ydim) for dt in range(tdim) if dy + dt > 0]
    ways = sorted(ways, key=hops, reverse=True)

    def send_pieces(among):
        for dy, dt in ways:
            l = lax.rem(t + dt, tdim)
            for size, has in sized(l, among):
                @pl.when(has)
                def _(dy=dy, l=l, size=size):
                    send_piece(lax.rem(y + dy, ydim), l, size)

    grad_all[...] = gradient(0, 256)
    for other in range(ydim):
        for dy in range(3):
            block = grad_all[96 * dy + out_rows * other : 96 * dy + out_rows * (other + 1), :]
            for half in range(2):
                start = block_rows * other + out_rows * (3 * half + dy)
                pieces[start : start + out_rows, :] = block[:, 128 * half : 128 * half + 128].astype(BF)
    send_pieces(range(6))

    grad_all[:, :32] = gradient(256, 288)
    for other in range(ydim):
        tails = [grad_all[96 * dy + out_rows * other : 96 * dy + out_rows * (other + 1), :32] for dy in range(3)]
        tails.append(jnp.zeros_like(tails[0]))
        start = block_rows * other + 6 * out_rows
        pieces[start : start + out_rows, :] = jnp.concatenate(tails, axis=1).astype(BF)
    send_pieces(range(6, 8))

    for half in range(2):
        for h in range(2):
            rows = [lat_dense[16 * half + 8 * h + i] for i in range(8)]
            for i, row in enumerate(swap_blocks(rows, lane)):
                lat_tiles[8 * half + i, :, 128 * h : 128 * h + 128] = row.astype(BF)
    for k in range(12):
        held = lat_tiles[tiles_ref[0, k]]
        lat_ref[k] = jnp.where(k < count, held, jnp.zeros_like(held))

    for cond, make in pend:
        @pl.when(cond)
        def _(make=make):
            make().wait_send()

    @pl.loop(0, tdim - 1)
    def _(f):
        @pl.when(t != f + 1)
        def _():
            arrived(ctx_out.at[f], ctx_send.at[f])

        @pl.when((t == 0) | (t == tdim - 1))
        def _():
            arrived(ctx_out.at[f, 0], ctx_edge_send.at[f])

    def add_up(size):
        start = owned_from(t)
        mine = pl.ds(start, size)
        used = pl.ds(0, size)
        parts[spot, used] = pieces[pl.ds(block_rows * y + start, size)]
        arrived(parts.at[pl.ds(0, plane - 1), used], piece_recv)
        total = parts[0, used].astype(F32)
        for i in range(1, plane):
            total = total + parts[i, used].astype(F32)
        z_in[b, used] = total.astype(BF)
        for d in sorted(range(1, zdim), key=lambda d: -min(d, zdim - d)):
            remote(
                z_in.at[b, used], z_in.at[b, used], z_send.at[d], z_recv, tile=lax.rem(b + d, zdim)
            ).start()
        arrived(pieces.at[pl.ds(0, block_rows * ydim - size)], piece_send)
        arrived(z_in.at[pl.ds(0, zdim - 1), used], z_recv)
        total = z_in[0, used].astype(F32)
        for i in range(1, zdim):
            total = total + z_in[i, used].astype(F32)
        final[mine] = total.astype(BF)
        for d in range(1, tdim):
            remote(
                final.at[mine], final.at[mine], final_send.at[d - 1], final_recv.at[t], tm=lax.rem(t + d, tdim)
            ).start()
        for d in range(1, zdim):
            arrived(z_in.at[b, used], z_send.at[d])

    for size, has in sized(t, range(8)):
        @pl.when(has)
        def _(size=size):
            add_up(size)

    for l in range(8):
        @pl.when(t != l)
        def _():
            arrived(final.at[pl.ds(sum(shared[:l]), shared[l])], final_recv.at[l])

    whole = final[...].astype(F32)
    for dy in range(3):
        at = [out_rows * dy, out_rows * (3 + dy), out_rows * 6]
        columns = [whole[a : a + out_rows, :] for a in at]
        columns[2] = columns[2][:, 32 * dy : 32 * (dy + 1)]
        grad_ref[:, 288 * dy : 288 * (dy + 1)] = jnp.concatenate(columns, axis=1)

    for size, has in sized(t, range(8)):
        @pl.when(has)
        def _(size=size):
            for d in range(1, tdim):
                arrived(final.at[pl.ds(0, size)], final_send.at[d - 1])


def body(sizes, frames_in, w_in, gate_bias, w_ent, active_tiles, active_count, cotangent):
    ydim, tdim, zdim = sizes
    plane = ydim * tdim
    per = 32 // tdim
    out_rows = 96 // ydim
    shared = shares(out_rows)
    vmem = pl.BlockSpec(memory_space=pltpu.VMEM)
    hbm = pl.BlockSpec(memory_space=pltpu.HBM)
    dma = pltpu.SemaphoreType.DMA
    latent, grad = pl.pallas_call(
        functools.partial(kernel, sizes),
        out_shape=(
            jax.ShapeDtypeStruct((12, 48, 256), BF),
            jax.ShapeDtypeStruct((out_rows, 864), F32),
        ),
        in_specs=[hbm] * 7,
        out_specs=(vmem, vmem),
        scratch_shapes=[
            pltpu.VMEM((96, 432), BF),
            pltpu.VMEM((1, 48), F32),
            pltpu.VMEM((96, 864), BF),
            pltpu.SMEM((1, 12), jnp.int32),
            pltpu.SMEM((1, 1, 1), jnp.int32),
            pltpu.VMEM((48, 32, 128), BF),
            pltpu.VMEM((48 * 32, 128), F32),
            pltpu.VMEM((34, 48, 128), BF),
            pltpu.VMEM((12, 48, 256), BF),
            pltpu.VMEM((tdim, per + 2, 48, 128), BF),
            pltpu.VMEM((tdim, 48, 128), BF),
            pltpu.VMEM((2, 48, 128), BF),
            pltpu.VMEM(((per + 2) * 144, 128), BF),
            pltpu.VMEM((tdim - 1, 48, per * 128), F32),
            pltpu.VMEM((tdim - 1, 48, per * 128), F32),
            pltpu.VMEM((48, per * 128), F32),
            pltpu.VMEM((tdim - 1, per, 48, 128), BF),
            pltpu.VMEM((34, 48, 128), BF),
            pltpu.VMEM((2, 48, 128), BF),
            pltpu.VMEM((2, 96, 432), BF),
            pltpu.VMEM((2, 96, 2048), F32),
            pltpu.VMEM((34 * 288, 128), BF),
            pltpu.VMEM((32, 48, 128), F32),
            pltpu.VMEM((36 * 96, 128), BF),
            pltpu.VMEM((32, 48, 128), F32),
            pltpu.VMEM((16, 48, 256), BF),
            pltpu.VMEM((288, 256), F32),
            pltpu.VMEM((ydim * sum(shared), 128), BF),
            pltpu.VMEM((plane, max(shared), 128), BF),
            pltpu.VMEM((zdim, max(shared), 128), BF),
            pltpu.VMEM((sum(shared), 128), BF),
            dma((7,)),
            dma((tdim,)), dma((tdim,)),
            dma((2,)), dma((tdim,)),
            dma((2,)), dma((2,)),
            dma((tdim - 1,)), dma((tdim,)),
            dma((tdim - 1,)), dma((2,)),
            dma, dma,
            dma((zdim,)), dma,
            dma((tdim - 1,)), dma((tdim,)),
            pltpu.SemaphoreType.REGULAR((len(relay_strides(zdim)) + 1,)),
        ],
        compiler_params=pltpu.CompilerParams(
            collective_id=0, has_side_effects=True, vmem_limit_bytes=32 * 1024 * 1024
        ),
        cost_estimate=pl.CostEstimate(flops=1_700_000_000, bytes_accessed=1_500_000, transcendentals=1_500_000),
        name="coding_window",
    )(
        pltpu.with_memory_space_constraint(frames_in[0, 0], pltpu.HBM),
        pltpu.with_memory_space_constraint(w_in, pltpu.HBM),
        pltpu.with_memory_space_constraint(gate_bias[None], pltpu.HBM),
        pltpu.with_memory_space_constraint(w_ent, pltpu.HBM),
        pltpu.with_memory_space_constraint(active_tiles[0, 0], pltpu.HBM),
        active_count,
        pltpu.with_memory_space_constraint(cotangent[0, 0, 0], pltpu.HBM),
    )
    return (latent[None, None, None], grad)


def solution(mesh):
    sizes = tuple(mesh.shape[axis] for axis in ("dp", "tm", "tile"))
    return jax.shard_map(
        functools.partial(body, sizes),
        mesh=mesh,
        in_specs=(
            P("dp", "tm", None, "tile", None),
            P(),
            P(),
            P(),
            P("dp", "tm", "tile", None),
            P("dp", "tm", "tile"),
            P("dp", "tm", "tile", None, None, None),
        ),
        out_specs=(P("dp", "tm", "tile", None, None, None), P("dp", None)),
        check_vma=False,
    )
```
